256 devices in a mesh: ctx: 32 (over y, z), tp: 8 (over x, core).
Axes of the slice: x: 4, y: 4, z: 8, core: 2. Of those that a mesh axis runs over, the one named last changes fastest.
Arguments:
- qkv: bfloat16 [32768, 3, 8192], P(('ctx', 'tp')), may hold values from -60 to 60
- gain: float32 [8192], replicated, may hold values from 0.1 to 1.9
Outputs:
- normed: bfloat16 [32768, 8192], P(('ctx', 'tp'))
The draws below stay inside these ranges and needn't reach their ends.
All inputs are finite; a program needn't handle non-finite values.
Results may differ from the reference program's by a relative error of at most 0.015.
Values may be sent and summed in bfloat16 or wider, within the bound.
No kernel may reach another device: no remote copies, remote signals or barrier semaphores. Data moves between devices by JAX's collectives and lax.ppermute only.
A program may use at most 128 MiB of HBM per device.

```python
import math
import jax
import jax.numpy as jnp
from jax import lax

H = 64
DH = 128
STRETCH = 256
SEQ = 32768


def draw_qkv(key, part):
    key = jax.random.fold_in(key, 11)
    key_base, key_rows, key_cols = jax.random.split(key, 3)
    shape = (SEQ, 3, H * DH)
    base = jnp.clip(jax.random.normal(key_base, shape, jnp.float32), -6.0, 6.0)
    spread = math.log(10.0)
    row_scale = jnp.exp(spread * jax.random.uniform(key_rows, (SEQ, 1, 1), jnp.float32))
    col_scale = jnp.exp(math.log(10.0) * jax.random.uniform(key_cols, (1, 1, H * DH), jnp.float32))
    which = jnp.arange(3)[None, :, None]
    scale = jnp.where(which == 0, row_scale, jnp.float32(1.0))
    scale = scale * jnp.where(which == 2, col_scale, jnp.float32(1.0))
    return (base * scale).astype(jnp.bfloat16)


def setup_inputs(seed: int = 0) -> dict:
    seeds = jax.random.split(jax.random.key(seed), 3)
    return {
        "qkv": draw_qkv(jax.random.fold_in(seeds[2], 71), 0),
        "gain": jnp.clip(1.0 + 0.18 * jax.random.normal(seeds[1], (H * DH,), jnp.float32), 0.1, 1.9),
    }


def one_head(qkv, index):
    seq = qkv.shape[0]
    nblock = seq // STRETCH
    cols = lax.dynamic_slice_in_dim(qkv, (index * DH).astype(jnp.int32), DH, 2)
    query_rows = cols[:, 0].astype(jnp.float32).reshape(nblock, STRETCH, DH)
    keys = cols[:, 1].astype(jnp.float32).reshape(nblock, STRETCH, DH)
    value_rows = cols[:, 2].astype(jnp.float32).reshape(nblock, STRETCH, DH)
    states = jnp.einsum('ncd,nce->nde', keys, value_rows)
    earlier = jnp.cumsum(states, 0) - states
    prior_state_sum = lax.optimization_barrier(earlier.astype(jnp.bfloat16)).astype(jnp.float32)
    score_matrix = jnp.einsum('nid,njd->nij', query_rows, keys)
    rows = lax.broadcasted_iota(jnp.int32, (STRETCH, STRETCH), 0)
    cols_i = lax.broadcasted_iota(jnp.int32, (STRETCH, STRETCH), 1)
    score_matrix = jnp.where((cols_i <= rows)[None], score_matrix, jnp.float32(0.0))
    score_matrix = lax.optimization_barrier(score_matrix.astype(jnp.bfloat16)).astype(jnp.float32)
    attended_output = jnp.einsum('ugh,uhc->ugc', score_matrix, value_rows) + jnp.einsum('lmp,lpo->lmo', query_rows, prior_state_sum)
    return attended_output.astype(jnp.bfloat16).reshape(seq, DH)

def reference(qkv, gain):
    seq = qkv.shape[0]
    heads = lax.map(lambda index: one_head(qkv, index), jnp.arange(H, dtype=jnp.int32))
    attended_output = jnp.transpose(heads, (1, 0, 2)).reshape(seq, H * DH)
    value_rows = attended_output.astype(jnp.float32)
    meansq = lax.optimization_barrier(jnp.mean(value_rows * value_rows, axis=-1, keepdims=True))
    return (value_rows * lax.rsqrt(meansq + 1e-06) * gain[None, :]).astype(jnp.bfloat16)
```

```python
import functools

import jax
import jax.numpy as jnp
from jax import lax
from jax.experimental import pallas as pl
from jax.experimental.pallas import tpu as pltpu
from jax.sharding import PartitionSpec as P

DH = 128
F32 = jnp.float32
BF16 = jnp.bfloat16


def cost(flops, nbytes):
    return pl.CostEstimate(flops=flops, bytes_accessed=nbytes, transcendentals=0)


def head_state(keys, value_rows, h):
    cols = pl.ds(h * DH, DH)
    return lax.dot_general(
        keys[:, cols], value_rows[:, cols], (((0,), (0,)), ((), ())), preferred_element_type=F32
    )


def send_states_body(place, k_ref, v_ref, out_ref):
    for h in range(out_ref.shape[0]):
        out_ref[h] = head_state(k_ref, v_ref, h).astype(BF16)


def chip_states_body(place, k_ref, v_ref, got_ref, first_ref, *chip_refs):
    step = pl.program_id(0)
    core = place[1]
    for piece, chip_ref in enumerate(chip_refs):

        @pl.when(step == piece)
        def _():
            for h in range(chip_ref.shape[0]):
                mine = head_state(k_ref, v_ref, h)
                got = got_ref[h]
                chip_ref[h] = (mine + got.astype(F32)).astype(BF16)
                first_ref[h] = jnp.where(core == 0, mine.astype(BF16), got)


def inside_body(place, q_ref, k_ref, v_ref, out_ref):
    rows = q_ref.shape[0]
    allowed = lax.broadcasted_iota(jnp.int32, (rows, rows), 1) <= lax.broadcasted_iota(
        jnp.int32, (rows, rows), 0
    )
    for h in range(q_ref.shape[1] // DH):
        cols = pl.ds(h * DH, DH)
        scores = lax.dot_general(
            q_ref[:, cols], k_ref[:, cols], (((1,), (1,)), ((), ())), preferred_element_type=F32
        )
        scores = jnp.where(allowed, scores, 0.0).astype(BF16)
        out_ref[:, cols] = jnp.dot(scores, v_ref[:, cols], preferred_element_type=F32)


def running_sum_body(x_ref, out_ref):
    def one(i, acc):
        out_ref[i] = acc.astype(BF16)
        return acc + x_ref[i].astype(F32)

    lax.fori_loop(0, x_ref.shape[0], one, jnp.zeros(x_ref.shape[1:], F32), unroll=True)


def chip_priors_body(place, base_ref, *refs):
    n = len(refs) // 2
    chips, outs = refs[:n], refs[n:]
    x = place[0]
    where = [lax.rem(x - d + n, n) for d in range(n)]
    base = base_ref[...].astype(F32)
    terms = [c[...].astype(F32) for c in chips]
    for d in range(n):
        acc = base
        for e in range(n):
            if e != d:
                acc = acc + jnp.where(where[e] < where[d], terms[e], 0.0)
        outs[d][...] = acc.astype(BF16)


def core_priors_body(place, first_ref, *refs):
    n = len(refs) - 2
    parts, keep_ref, send_ref = refs[:n], refs[n], refs[n + 1]
    step = pl.program_id(0)
    core = place[1]
    for piece, part in enumerate(parts):

        @pl.when(step == piece)
        def _():
            prior = part[...]
            later = (prior.astype(F32) + first_ref[...].astype(F32)).astype(BF16)
            keep_ref[...] = jnp.where(core == 0, prior, later)
            send_ref[...] = jnp.where(core == 0, later, prior)


def attend_body(place, q_ref, inside_ref, prior_ref, out_ref, sq_ref):
    total = jnp.zeros((q_ref.shape[0], DH), F32)
    for h in range(q_ref.shape[1] // DH):
        cols = pl.ds(h * DH, DH)
        value = inside_ref[:, cols] + jnp.dot(
            q_ref[:, cols], prior_ref[h], preferred_element_type=F32
        )
        value = value.astype(BF16)
        out_ref[:, cols] = value
        value = value.astype(F32)
        total = total + value * value

    @pl.when(pl.program_id(0) == 0)
    def _():
        sq_ref[...] = total

    @pl.when(pl.program_id(0) > 0)
    def _():
        sq_ref[...] += total


def finish_body(nx, place, q_ref, inside_ref, prior_ref, kept_ref, sq_ref, gain_ref, out_ref, sum_ref):
    step = pl.program_id(0)
    core = place[1]
    width = q_ref.shape[1]
    group = (1 - core) * nx + lax.rem(place[0] + step, nx)

    @pl.when(step == 0)
    def _():
        sum_ref[...] = sq_ref[...]

    total = jnp.zeros((q_ref.shape[0], DH), F32)
    for h in range(width // DH):
        cols = pl.ds(h * DH, DH)
        value = inside_ref[:, cols] + jnp.dot(
            q_ref[:, cols], prior_ref[h], preferred_element_type=F32
        )
        value = value.astype(BF16)
        out_ref[:, pl.ds(pl.multiple_of(group * width + h * DH, DH), DH)] = value
        value = value.astype(F32)
        total = total + value * value
    sum_ref[...] += total

    @pl.when(step == nx - 1)
    def _():
        meansq = jnp.sum(sum_ref[...], axis=-1, keepdims=True) / out_ref.shape[1]
        scale = lax.rsqrt(meansq + 1e-06)
        for piece in range(nx):
            mine = pl.multiple_of((core * nx + lax.rem(place[0] + piece, nx)) * width, width)
            other = pl.multiple_of(((1 - core) * nx + piece) * width, width)
            for h in range(width // DH):
                cols = pl.ds(mine + h * DH, DH)
                value = kept_ref[:, pl.ds(piece * width + h * DH, DH)].astype(F32)
                out_ref[:, cols] = (value * scale * gain_ref[:, cols]).astype(BF16)
                cols = pl.ds(other + h * DH, DH)
                value = out_ref[:, cols].astype(F32)
                out_ref[:, cols] = (value * scale * gain_ref[:, cols]).astype(BF16)


def per_device(nx, nctx, qkv, gain):
    rows, _, width = qkv.shape
    heads = width // DH
    half = heads // 2
    each = half // nx
    block = each * DH
    tp = lax.axis_index("tp")
    place = jnp.stack([tp // 2, lax.rem(tp, 2)]).astype(jnp.int32)
    rolled = jnp.transpose(qkv, (1, 0, 2))
    swap = [(i, i ^ 1) for i in range(2 * nx)]

    def shift(d):
        return [(2 * x + c, 2 * ((x + d) % nx) + c) for x in range(nx) for c in range(2)]

    def columns(which, own):
        def index(i, place):
            side = place[1] if own else 1 - place[1]
            return (which, 0, side * nx + lax.rem(place[0] + i, nx))

        return pl.BlockSpec((None, rows, block), index)

    def flat(own):
        def index(i, place):
            side = place[1] if own else 1 - place[1]
            return (0, side * nx + lax.rem(place[0] + i, nx))

        return pl.BlockSpec((rows, block), index)

    by_step = pl.BlockSpec((each, DH, DH), lambda i, place: (i, 0, 0))
    fixed = pl.BlockSpec((each, DH, DH), lambda i, place: (0, 0, 0))
    half_states = jax.ShapeDtypeStruct((half, DH, DH), BF16)
    part_states = jax.ShapeDtypeStruct((each, DH, DH), BF16)

    def call(body, grid, in_specs, out_specs, out_shape, scratch=(), cost_estimate=None):
        return pl.pallas_call(
            body,
            grid_spec=pltpu.PrefetchScalarGridSpec(
                num_scalar_prefetch=1,
                grid=grid,
                in_specs=in_specs,
                out_specs=out_specs,
                scratch_shapes=scratch,
            ),
            out_shape=out_shape,
            cost_estimate=cost_estimate,
            compiler_params=pltpu.CompilerParams(vmem_limit_bytes=40 * 2**20),
        )

    flops = 2 * half * rows * DH * DH
    send = call(
        send_states_body,
        (nx,),
        [columns(1, False), columns(2, False)],
        by_step,
        half_states,
        cost_estimate=cost(flops, 3 * 2**20),
    )(place, rolled, rolled)
    got = lax.ppermute(send, "tp", swap)
    first, *chips = call(
        chip_states_body,
        (nx,),
        [columns(1, True), columns(2, True), by_step],
        [by_step] + [fixed] * nx,
        [half_states] + [part_states] * nx,
        cost_estimate=cost(flops, 5 * 2**20),
    )(place, rolled, rolled, got)
    chips = [chips[0]] + [lax.ppermute(chips[d], "tp", shift(d)) for d in range(1, nx)]

    inside = call(
        inside_body,
        (2 * nx,),
        [pl.BlockSpec((None, rows, block), lambda i, place, w=w: (w, 0, i)) for w in range(3)],
        pl.BlockSpec((rows, block), lambda i, place: (0, i)),
        jax.ShapeDtypeStruct((rows, width), F32),
        cost_estimate=cost(4 * flops, 10 * 2**20),
    )(place, rolled, rolled, rolled)

    total = sum(c.astype(F32) for c in chips).astype(BF16)
    piece = each * DH // nctx
    spread = lax.all_to_all(
        total.reshape(nctx, piece, DH), "ctx", split_axis=0, concat_axis=0, tiled=True
    )
    spread = pl.pallas_call(
        running_sum_body, out_shape=jax.ShapeDtypeStruct(spread.shape, BF16)
    )(spread)
    base = lax.all_to_all(spread, "ctx", split_axis=0, concat_axis=0, tiled=True)
    base = base.reshape(each, DH, DH)

    two = pl.BlockSpec((2, DH, DH), lambda i, place: (i, 0, 0))
    parts = call(
        chip_priors_body,
        (each // 2,),
        [two] * (nx + 1),
        [two] * nx,
        [part_states] * nx,
        cost_estimate=cost(0, 3 * 2**20),
    )(place, base, *chips)
    parts = [parts[0]] + [lax.ppermute(parts[d], "tp", shift(-d)) for d in range(1, nx)]
    keep, give = call(
        core_priors_body,
        (nx,),
        [by_step] + [fixed] * nx,
        [by_step, by_step],
        [half_states, half_states],
        cost_estimate=cost(0, 4 * 2**20),
    )(place, first, *parts)
    other = lax.ppermute(give, "tp", swap)

    kept, sq = call(
        attend_body,
        (nx,),
        [columns(0, True), flat(True), by_step],
        [
            pl.BlockSpec((rows, block), lambda i, place: (0, i)),
            pl.BlockSpec((rows, DH), lambda i, place: (0, 0)),
        ],
        [jax.ShapeDtypeStruct((rows, width // 2), BF16), jax.ShapeDtypeStruct((rows, DH), F32)],
        cost_estimate=cost(flops, 5 * 2**20),
    )(place, rolled, inside, keep)
    return call(
        functools.partial(finish_body, nx),
        (nx,),
        [
            columns(0, False),
            flat(False),
            by_step,
            pl.BlockSpec((rows, width // 2), lambda i, place: (0, 0)),
            pl.BlockSpec((rows, DH), lambda i, place: (0, 0)),
            pl.BlockSpec((1, width), lambda i, place: (0, 0)),
        ],
        pl.BlockSpec((rows, width), lambda i, place: (0, 0)),
        jax.ShapeDtypeStruct((rows, width), BF16),
        scratch=[pltpu.VMEM((rows, DH), F32)],
        cost_estimate=cost(flops, 7 * 2**20),
    )(place, rolled, inside, other, kept, sq, gain.reshape(1, width))


def solution(mesh):
    return jax.shard_map(
        functools.partial(per_device, mesh.shape["tp"] // 2, mesh.shape["ctx"]),
        mesh=mesh,
        in_specs=(P(("ctx", "tp"), None, None), P()),
        out_specs=P(("ctx", "tp"), None),
        check_vma=False,
    )
```

```python
import functools

import jax
import jax.numpy as jnp
from jax import lax
from jax.experimental import pallas as pl
from jax.experimental.pallas import tpu as pltpu
from jax.sharding import PartitionSpec as P

DH = 128
F32 = jnp.float32
BF16 = jnp.bfloat16
VMEM = pl.BlockSpec(memory_space=pltpu.VMEM)
SMEM = pl.BlockSpec(memory_space=pltpu.SMEM)
HBM = pl.BlockSpec(memory_space=pltpu.HBM)


def head_state(keys, value_rows):
    return lax.dot_general(
        keys, value_rows, (((0,), (0,)), ((), ())), preferred_element_type=F32
    )


def send_states_body(place, qkv_ref, out_ref, k_buf, v_buf, sems):
    n, _, block = k_buf.shape
    each = block // DH
    first = (1 - place[1]) * n
    copies = []
    for i in range(n):
        cols = pl.ds(pl.multiple_of((first + i) * block, block), block)
        pair = []
        for which, buf in ((1, k_buf), (2, v_buf)):
            copy = pltpu.make_async_copy(
                qkv_ref.at[which, :, cols], buf.at[i], sems.at[which - 1, i]
            )
            copy.start()
            pair.append(copy)
        copies.append(pair)
    for i in range(n):
        for copy in copies[i]:
            copy.wait()
        for h in range(each):
            cols = pl.ds(h * DH, DH)
            out_ref[i * each + h] = head_state(k_buf[i, :, cols], v_buf[i, :, cols]).astype(BF16)


def own_states_body(place, qkv_ref, out_ref):
    half = out_ref.shape[0]
    first = place[1] * half
    for h in range(half):
        cols = pl.ds(pl.multiple_of((first + h) * DH, DH), DH)
        out_ref[h] = head_state(qkv_ref[1, :, cols], qkv_ref[2, :, cols])


def chip_states_body(place, own_ref, got_ref, *chip_refs):
    n = len(chip_refs)
    each = chip_refs[0].shape[0]
    for d in range(n):
        first = lax.rem(place[0] + d, n) * each
        for h in range(each):
            chip_refs[d][h] = (own_ref[first + h] + got_ref[first + h].astype(F32)).astype(BF16)


def scores_body(place, qkv_ref, own_ref, got_ref, out_ref, first_ref):
    rows = out_ref.shape[0]
    allowed = lax.broadcasted_iota(jnp.int32, (rows, rows), 1) <= lax.broadcasted_iota(
        jnp.int32, (rows, rows), 0
    )
    for h in range(out_ref.shape[1] // DH):
        cols = pl.ds(h * DH, DH)
        scores = lax.dot_general(
            qkv_ref[0, :, cols],
            qkv_ref[1, :, cols],
            (((1,), (1,)), ((), ())),
            preferred_element_type=F32,
        )
        out_ref[:, cols] = jnp.where(allowed, scores, 0.0).astype(BF16)

    @pl.when(place[1] == 0)
    def _():
        first_ref[...] = own_ref[...].astype(BF16)

    @pl.when(place[1] != 0)
    def _():
        first_ref[...] = got_ref[...]


def running_sum_body(x_ref, out_ref):
    acc = jnp.zeros(x_ref.shape[1:], F32)
    for i in range(x_ref.shape[0]):
        out_ref[i] = acc.astype(BF16)
        acc = acc + x_ref[i].astype(F32)


def chip_priors_body(place, base_ref, *refs):
    n = len(refs) // 2
    chips, outs = refs[:n], refs[n:]
    x = place[0]
    where = [lax.rem(x - d + n, n) for d in range(n)]
    weight = [
        [None if e == d else jnp.where(where[e] < where[d], 1.0, 0.0) for e in range(n)]
        for d in range(n)
    ]
    for h in range(base_ref.shape[0]):
        base = base_ref[h].astype(F32)
        terms = [c[h].astype(F32) for c in chips]
        for d in range(n):
            acc = base
            for e in range(n):
                if e != d:
                    acc = acc + terms[e] * weight[d][e]
            outs[d][h] = acc.astype(BF16)


def core_priors_body(place, first_ref, *refs):
    n = len(refs) - 2
    parts, keep_ref, send_ref = refs[:n], refs[n], refs[n + 1]
    each = parts[0].shape[0]

    def fill(early, late):
        for d in range(n):
            group = lax.rem(place[0] + d, n) * each
            for h in range(each):
                prior = parts[d][h]
                early[group + h] = prior
                late[group + h] = (prior.astype(F32) + first_ref[group + h].astype(F32)).astype(BF16)

    @pl.when(place[1] == 0)
    def _():
        fill(keep_ref, send_ref)

    @pl.when(place[1] != 0)
    def _():
        fill(send_ref, keep_ref)


def attend(scores_ref, qkv_ref, prior_ref, first, h):
    cols = pl.ds(pl.multiple_of((first + h) * DH, DH), DH)
    left = jnp.concatenate([scores_ref[:, cols], qkv_ref[0, :, cols]], axis=1)
    right = jnp.concatenate([qkv_ref[2, :, cols], prior_ref[h]], axis=0)
    return jnp.dot(left, right, preferred_element_type=F32).astype(BF16)


def attend_body(place, qkv_ref, scores_ref, prior_ref, out_ref, sq_ref):
    half = prior_ref.shape[0]
    total = jnp.zeros(sq_ref.shape, F32)
    for h in range(half):
        value = attend(scores_ref, qkv_ref, prior_ref, place[1] * half, h)
        out_ref[:, pl.ds(h * DH, DH)] = value
        value = value.astype(F32)
        total = total + value * value
    sq_ref[...] = total


def finish_body(
    place, qkv_ref, scores_ref, prior_ref, kept_ref, sq_ref, gain_ref, out_ref, other, done, sems
):
    half = prior_ref.shape[0]
    mine, others = place[1] * half, (1 - place[1]) * half
    total = sq_ref[...]
    for h in range(half):
        value = attend(scores_ref, qkv_ref, prior_ref, others, h)
        other[:, pl.ds(h * DH, DH)] = value
        value = value.astype(F32)
        total = total + value * value
    meansq = jnp.sum(total, axis=-1, keepdims=True) / out_ref.shape[1]
    scale = jnp.broadcast_to(lax.rsqrt(meansq + 1e-06), total.shape)
    each = half // (sems.shape[0] // 2)
    copies = []
    for source, first in ((kept_ref, mine), (other, others)):
        for start in range(0, half, each):
            slot = len(copies)
            for h in range(start, start + each):
                cols = pl.ds(h * DH, DH)
                gain = gain_ref[:, pl.ds(pl.multiple_of((first + h) * DH, DH), DH)]
                value = source[:, cols].astype(F32)
                done[slot, :, pl.ds((h - start) * DH, DH)] = (value * scale * gain).astype(BF16)
            wide = each * DH
            cols = pl.ds(pl.multiple_of((first + start) * DH, wide), wide)
            copy = pltpu.make_async_copy(done.at[slot], out_ref.at[:, cols], sems.at[slot])
            copy.start()
            copies.append(copy)
    for copy in copies:
        copy.wait()


def per_device(nx, nctx, qkv, gain):
    rows, _, width = qkv.shape
    heads = width // DH
    half = heads // 2
    each = half // nx
    block = each * DH
    tp = lax.axis_index("tp")
    place = jnp.stack([tp // 2, lax.rem(tp, 2)]).astype(jnp.int32)
    qkv = jnp.transpose(qkv, (1, 0, 2))
    swap = [(i, i ^ 1) for i in range(2 * nx)]

    def shift(d):
        return [(2 * x + c, 2 * ((x + d) % nx) + c) for x in range(nx) for c in range(2)]

    def states(n, dtype=BF16):
        return jax.ShapeDtypeStruct((n, DH, DH), dtype)

    def call(body, in_specs, out_specs, out_shape, flops, nbytes, scratch=(), limit=16):
        return pl.pallas_call(
            body,
            in_specs=in_specs,
            out_specs=out_specs,
            out_shape=out_shape,
            scratch_shapes=scratch,
            cost_estimate=pl.CostEstimate(flops=flops, bytes_accessed=nbytes, transcendentals=0),
            compiler_params=pltpu.CompilerParams(vmem_limit_bytes=limit * 2**20),
        )

    product = 2 * half * rows * DH * DH
    mib = 2**20
    send = call(
        send_states_body,
        [SMEM, HBM],
        VMEM,
        states(half),
        product,
        3 * mib,
        scratch=[
            pltpu.VMEM((nx, rows, block), BF16),
            pltpu.VMEM((nx, rows, block), BF16),
            pltpu.SemaphoreType.DMA((2, nx)),
        ],
    )(place, pltpu.with_memory_space_constraint(qkv, pltpu.HBM))
    got = lax.ppermute(send, "tp", swap)
    own = call(own_states_body, [SMEM, VMEM], VMEM, states(half, F32), product, 4 * mib)(place, qkv)
    chips = call(
        chip_states_body, [SMEM, VMEM, VMEM], [VMEM] * nx, [states(each)] * nx, 0, 4 * mib
    )(place, own, got)
    later, *chips = lax.optimization_barrier((place, *chips))
    chips = [chips[0]] + [lax.ppermute(chips[d], "tp", shift(d)) for d in range(1, nx)]
    scores, first = call(
        scores_body,
        [SMEM, VMEM, VMEM, VMEM],
        [VMEM, VMEM],
        [jax.ShapeDtypeStruct((rows, width), BF16), states(half)],
        2 * product,
        10 * mib,
    )(later, qkv, own, got)
    scores, first, *chips = lax.optimization_barrier((scores, first, *chips))

    total = sum(c.astype(F32) for c in chips).astype(BF16)
    piece = each * DH // nctx
    spread = lax.all_to_all(
        total.reshape(nctx, piece, DH), "ctx", split_axis=0, concat_axis=0, tiled=True
    )
    spread = call(
        running_sum_body, [VMEM], VMEM, jax.ShapeDtypeStruct(spread.shape, BF16), 0, mib
    )(spread)
    base = lax.all_to_all(spread, "ctx", split_axis=0, concat_axis=0, tiled=True)
    base = base.reshape(each, DH, DH)

    parts = call(
        chip_priors_body,
        [SMEM] + [VMEM] * (nx + 1),
        [VMEM] * nx,
        [states(each)] * nx,
        0,
        3 * mib,
    )(place, base, *chips)
    parts = [parts[0]] + [lax.ppermute(parts[d], "tp", shift(-d)) for d in range(1, nx)]
    keep, give = call(
        core_priors_body,
        [SMEM] + [VMEM] * (nx + 1),
        [VMEM, VMEM],
        [states(half)] * 2,
        0,
        4 * mib,
    )(place, first, *parts)
    other = lax.ppermute(give, "tp", swap)

    kept, sq = call(
        attend_body,
        [SMEM] + [VMEM] * 3,
        [VMEM, VMEM],
        [jax.ShapeDtypeStruct((rows, width // 2), BF16), jax.ShapeDtypeStruct((rows, DH), F32)],
        2 * product,
        5 * mib,
    )(place, qkv, scores, keep)
    return call(
        finish_body,
        [SMEM] + [VMEM] * 6,
        HBM,
        jax.ShapeDtypeStruct((rows, width), BF16),
        2 * product,
        7 * mib,
        scratch=[
            pltpu.VMEM((rows, width // 2), BF16),
            pltpu.VMEM((2 * nx, rows, block), BF16),
            pltpu.SemaphoreType.DMA((2 * nx,)),
        ],
    )(place, qkv, scores, other, kept, sq, gain.reshape(1, width))


def solution(mesh):
    return jax.shard_map(
        functools.partial(per_device, mesh.shape["tp"] // 2, mesh.shape["ctx"]),
        mesh=mesh,
        in_specs=(P(("ctx", "tp"), None, None), P()),
        out_specs=P(("ctx", "tp"), None),
        check_vma=False,
    )
```

```python
import functools

import jax
import jax.numpy as jnp
from jax import lax
from jax.experimental import pallas as pl
from jax.experimental.pallas import tpu as pltpu
from jax.sharding import PartitionSpec as P

DH = 128
F32 = jnp.float32
BF16 = jnp.bfloat16
VMEM = pl.BlockSpec(memory_space=pltpu.VMEM)
HBM = pl.BlockSpec(memory_space=pltpu.HBM)


ORDER = (2, 1, 3, 0)


def my_place():
    tp = lax.axis_index("tp")
    return tp // 2, lax.rem(tp, 2)


def group_of(place, d, n):
    return lax.rem(place[0] + d, n)


def columns(start, size):
    return pl.ds(pl.multiple_of(start, size), size)


def head_cols(h):
    return pl.ds(h * DH, DH)


def head_state(k_ref, v_ref, h):
    cols = head_cols(h)
    return lax.dot_general(
        k_ref[:, cols], v_ref[:, cols], (((0,), (0,)), ((), ())), preferred_element_type=F32
    )


def start_loads(qkv_ref, which, place, side, buf, sems):
    block = buf.shape[1] // len(ORDER)
    copies = []
    for i, d in enumerate(ORDER):
        start = (side * len(ORDER) + group_of(place, d, len(ORDER))) * block
        copy = pltpu.make_async_copy(
            qkv_ref.at[which, :, columns(start, block)],
            buf.at[:, pl.ds(i * block, block)],
            sems.at[i],
        )
        copy.start()
        copies.append(copy)
    return copies


def start_pairs(place, qkv_ref, side, k_ref, v_ref, sems):
    loads = [
        start_loads(qkv_ref, 1 + i, place, side, buf, sems.at[i])
        for i, buf in enumerate((k_ref, v_ref))
    ]
    return list(zip(*loads))


def first_body(qkv_ref, send_ref, k_ref, v_ref, own_k_ref, own_v_ref, sems):
    place = my_place()
    pairs = start_pairs(place, qkv_ref, 1 - place[1], k_ref, v_ref, sems.at[0])
    later = start_pairs(place, qkv_ref, place[1], own_k_ref, own_v_ref, sems.at[1])
    each = send_ref.shape[0] // len(pairs)
    for i, pair in enumerate(pairs):
        for copy in pair:
            copy.wait()
        for h in range(i * each, (i + 1) * each):
            send_ref[h] = head_state(k_ref, v_ref, h).astype(BF16)
    for pair in later:
        for copy in pair:
            copy.wait()


def own_body(k_ref, v_ref, own_ref, low_ref):
    for h in range(own_ref.shape[0]):
        state = head_state(k_ref, v_ref, h)
        own_ref[h] = state
        low_ref[h] = state.astype(BF16)


def chip_body(own_ref, got_ref, *chip_refs):
    each = chip_refs[0].shape[0]
    for i, chip_ref in enumerate(chip_refs):
        for h in range(each):
            at = i * each + h
            chip_ref[h] = (own_ref[at] + got_ref[at].astype(F32)).astype(BF16)


def inside_body(qkv_ref, *refs):
    place = my_place()
    kv_refs = refs[:4]
    got_ref, gain_ref, inside_ref, q_ref, order_ref, scores_ref, sems = refs[4:]
    rows, width = kv_refs[0].shape
    loads = [
        start_loads(qkv_ref, 0, place, side, q_ref.at[i], sems.at[i])
        for i, side in enumerate((place[1], 1 - place[1]))
    ]
    allowed = lax.broadcasted_iota(jnp.int32, (rows, rows), 1) <= lax.broadcasted_iota(
        jnp.int32, (rows, rows), 0
    )
    each = width // DH // len(ORDER)
    for side in range(2):
        for i in range(len(ORDER)):
            loads[side][i].wait()
            for h in range(i * each, (i + 1) * each):
                cols = head_cols(h)
                scores = lax.dot_general(
                    q_ref[side, :, cols],
                    kv_refs[2 * side][:, cols],
                    (((1,), (1,)), ((), ())),
                    preferred_element_type=F32,
                )
                scores_ref[side, :, cols] = jnp.where(allowed, scores, 0.0).astype(BF16)
    for i, side in enumerate((place[1], 1 - place[1])):
        block = each * DH
        for j, d in enumerate(ORDER):
            start = (side * len(ORDER) + group_of(place, d, len(ORDER))) * block
            order_ref[i, :, pl.ds(j * block, block)] = gain_ref[:, columns(start, block)]

    def plain(side):
        for h in range(width // DH):
            cols = head_cols(h)
            inside_ref[side, :, cols] = jnp.dot(
                scores_ref[side, :, cols],
                kv_refs[2 * side + 1][:, cols],
                preferred_element_type=F32,
            )

    plain(1)

    @pl.when(place[1] == 0)
    def _():
        plain(0)

    @pl.when(place[1] != 0)
    def _():
        for h in range(width // DH):
            cols = head_cols(h)
            inside_ref[0, :, cols] = jnp.dot(
                jnp.concatenate([scores_ref[0, :, cols], q_ref[0, :, cols]], axis=1),
                jnp.concatenate([kv_refs[1][:, cols], got_ref[h]], axis=0),
                preferred_element_type=F32,
            )


def running_sum_body(x_ref, out_ref):
    acc = jnp.zeros(x_ref.shape[1:], F32)
    for i in range(x_ref.shape[0]):
        out_ref[i] = acc.astype(BF16)
        acc = acc + x_ref[i].astype(F32)


def chip_priors_body(base_ref, *refs):
    place = my_place()
    n = len(refs) // 2
    chips, outs = refs[:n], refs[n:]
    for x in range(n):

        @pl.when(place[0] == x)
        def _():
            for h in range(base_ref.shape[0]):
                acc = base_ref[h].astype(F32)
                for chip in range(n):
                    i = ORDER.index((x - chip) % n)
                    outs[i][h] = acc.astype(BF16)
                    if chip < n - 1:
                        acc = acc + chips[i][h].astype(F32)


def give_body(first, prior_ref, low_ref, out_ref):
    place = my_place()

    @pl.when(place[1] == 0)
    def _():
        for h in range(out_ref.shape[0]):
            state = low_ref[first + h].astype(F32)
            out_ref[h] = (prior_ref[h].astype(F32) + state).astype(BF16)

    @pl.when(place[1] != 0)
    def _():
        out_ref[...] = prior_ref[...]


def attend(side, q_ref, inside_ref, gain_ref, priors, out_ref, total):
    each = priors[0].shape[0]
    for i, prior in enumerate(priors):
        for h in range(each):
            cols = head_cols(i * each + h)
            value = jnp.dot(q_ref[side, :, cols], prior[h], preferred_element_type=F32)
            value = (inside_ref[side, :, cols] + value).astype(BF16).astype(F32)
            out_ref[:, cols] = value * gain_ref[side, :, cols]
            total = total + value * value
    return total


def attend_body(q_ref, inside_ref, gain_ref, *refs):
    priors, out_ref, sq_ref = refs[:-2], refs[-2], refs[-1]
    zero = jnp.zeros(sq_ref.shape, F32)
    sq_ref[...] = attend(0, q_ref, inside_ref, gain_ref, priors, out_ref, zero)


def finish_body(q_ref, inside_ref, gain_ref, kept_ref, sq_ref, *refs):
    place = my_place()
    priors, (out_ref, other, done, sems) = refs[:-4], refs[-4:]
    n, each = len(priors), priors[0].shape[0]
    total = attend(1, q_ref, inside_ref, gain_ref, priors, other, sq_ref[...])
    meansq = jnp.sum(total, axis=-1, keepdims=True) / out_ref.shape[1]
    scale = jnp.broadcast_to(lax.rsqrt(meansq + 1e-06), total.shape)
    copies = []
    for source, side in ((kept_ref, place[1]), (other, 1 - place[1])):
        for i, d in enumerate(ORDER):
            slot = len(copies)
            for h in range(each):
                value = source[:, head_cols(i * each + h)]
                done[slot, :, head_cols(h)] = (value * scale).astype(BF16)
            first = (side * n + group_of(place, d, n)) * each
            copy = pltpu.make_async_copy(
                done.at[slot], out_ref.at[:, columns(first * DH, each * DH)], sems.at[slot]
            )
            copy.start()
            copies.append(copy)
    for copy in copies:
        copy.wait()


def per_device(nx, nctx, qkv, gain):
    rows, _, width = qkv.shape
    heads = width // DH
    half = heads // 2
    each = half // nx
    block = each * DH
    gain = gain.reshape(1, width)
    qkv = pltpu.with_memory_space_constraint(jnp.transpose(qkv, (1, 0, 2)), pltpu.HBM)
    swap = [(i, i ^ 1) for i in range(2 * nx)]

    def shift(d):
        return [(2 * x + c, 2 * ((x + d) % nx) + c) for x in range(nx) for c in range(2)]

    def states(n, dtype=BF16):
        return jax.ShapeDtypeStruct((n, DH, DH), dtype)

    def call(body, in_specs, out_specs, out_shape, products, nbytes, scratch=()):
        return pl.pallas_call(
            body,
            in_specs=in_specs,
            out_specs=out_specs,
            out_shape=out_shape,
            scratch_shapes=scratch,
            cost_estimate=pl.CostEstimate(
                flops=2 * products * rows * DH * DH, bytes_accessed=nbytes, transcendentals=0
            ),
            compiler_params=pltpu.CompilerParams(vmem_limit_bytes=16 * 2**20),
        )

    mib = 2**20
    matrix = jax.ShapeDtypeStruct((rows, width // 2), BF16)
    loads = pltpu.SemaphoreType.DMA((2, nx))
    send, keys, value_rows, own_keys, own_values = call(
        first_body,
        [HBM],
        [VMEM] * 5,
        [states(half)] + [matrix] * 4,
        half,
        5 * mib,
        scratch=[pltpu.SemaphoreType.DMA((2, 2, nx))],
    )(qkv)
    got = lax.ppermute(send, "tp", swap)
    own, low = call(
        own_body, [VMEM] * 2, [VMEM] * 2, [states(half, F32), states(half)], half, 5 * mib
    )(own_keys, own_values)
    chips = call(chip_body, [VMEM, VMEM], [VMEM] * nx, [states(each)] * nx, 0, 4 * mib)(own, got)
    chips = list(chips)
    gain, chips[-1] = lax.optimization_barrier((gain, chips[-1]))
    chips = [
        c if d == 0 else lax.ppermute(c, "tp", shift(d)) for d, c in zip(ORDER, chips)
    ]
    wide = (2, rows, width // 2)
    inside, queries, gains = call(
        inside_body,
        [HBM] + [VMEM] * 6,
        [VMEM] * 3,
        [
            jax.ShapeDtypeStruct(wide, F32),
            jax.ShapeDtypeStruct(wide, BF16),
            jax.ShapeDtypeStruct((2, 1, width // 2), F32),
        ],
        4 * half,
        12 * mib,
        scratch=[pltpu.VMEM(wide, BF16), loads],
    )(qkv, own_keys, own_values, keys, value_rows, got, gain)
    inside, queries, gains, *chips = lax.optimization_barrier((inside, queries, gains, *chips))

    total = sum(c.astype(F32) for c in chips).astype(BF16)
    piece = each * DH // nctx
    spread = lax.all_to_all(
        total.reshape(nctx, piece, DH), "ctx", split_axis=0, concat_axis=0, tiled=True
    )
    spread = call(
        running_sum_body, [VMEM], VMEM, jax.ShapeDtypeStruct(spread.shape, BF16), 0, mib
    )(spread)
    base = lax.all_to_all(spread, "ctx", split_axis=0, concat_axis=0, tiled=True)
    base = base.reshape(each, DH, DH)

    parts = call(
        chip_priors_body,
        [VMEM] * (nx + 1),
        [VMEM] * nx,
        [states(each)] * nx,
        0,
        2 * mib,
    )(base, *chips)
    parts = [
        p if d == 0 else lax.ppermute(p, "tp", shift(-d)) for d, p in zip(ORDER, parts)
    ]
    others = []
    for i, part in enumerate(parts):
        give = call(
            functools.partial(give_body, i * each),
            [VMEM, VMEM],
            VMEM,
            states(each),
            0,
            mib,
        )(part, low)
        others.append(lax.ppermute(give, "tp", swap))
    kept, sq = call(
        attend_body,
        [VMEM] * (3 + nx),
        [VMEM, VMEM],
        [jax.ShapeDtypeStruct((rows, width // 2), F32), jax.ShapeDtypeStruct((rows, DH), F32)],
        half,
        5 * mib,
    )(queries, inside, gains, *parts)
    return call(
        finish_body,
        [VMEM] * (5 + nx),
        HBM,
        jax.ShapeDtypeStruct((rows, width), BF16),
        half,
        7 * mib,
        scratch=[
            pltpu.VMEM((rows, width // 2), F32),
            pltpu.VMEM((2 * nx, rows, block), BF16),
            pltpu.SemaphoreType.DMA((2 * nx,)),
        ],
    )(queries, inside, gains, kept, sq, *others)


def solution(mesh):
    return jax.shard_map(
        functools.partial(per_device, mesh.shape["tp"] // 2, mesh.shape["ctx"]),
        mesh=mesh,
        in_specs=(P(("ctx", "tp"), None, None), P()),
        out_specs=P(("ctx", "tp"), None),
        check_vma=False,
    )
```

```python
import functools

import jax
import jax.numpy as jnp
from jax import lax
from jax.experimental import pallas as pl
from jax.experimental.pallas import tpu as pltpu
from jax.sharding import PartitionSpec as P

DH = 128
F32 = jnp.float32
BF16 = jnp.bfloat16
VMEM = pl.BlockSpec(memory_space=pltpu.VMEM)
HBM = pl.BlockSpec(memory_space=pltpu.HBM)


ORDER = (2, 1, 3, 0)
CHUNKS = 1
NZ = 8
LINE = NZ // 2


def my_place():
    tp = lax.axis_index("tp")
    return tp // 2, lax.rem(tp, 2)


def line_place():
    ctx = lax.axis_index("ctx")
    z = lax.rem(ctx, NZ)
    late = z >= LINE
    return ctx // NZ, late, jnp.where(late, NZ - 1 - z, z)


def quarter_of(m, d):
    return lax.rem(m + d, LINE)


def group_of(place, d, n):
    return lax.rem(place[0] + d, n)


def columns(start, size):
    return pl.ds(pl.multiple_of(start, size), size)


def head_cols(h):
    return pl.ds(h * DH, DH)


def head_state(k_ref, v_ref, h):
    cols = head_cols(h)
    return lax.dot_general(
        k_ref[:, cols], v_ref[:, cols], (((0,), (0,)), ((), ())), preferred_element_type=F32
    )


def start_loads(qkv_ref, which, place, side, buf, sems):
    block = buf.shape[1] // len(ORDER)
    copies = []
    for i, d in enumerate(ORDER):
        start = (side * len(ORDER) + group_of(place, d, len(ORDER))) * block
        copy = pltpu.make_async_copy(
            qkv_ref.at[which, :, columns(start, block)],
            buf.at[:, pl.ds(i * block, block)],
            sems.at[i],
        )
        copy.start()
        copies.append(copy)
    return copies


def start_pairs(place, qkv_ref, side, k_ref, v_ref, sems):
    loads = [
        start_loads(qkv_ref, 1 + i, place, side, buf, sems.at[i])
        for i, buf in enumerate((k_ref, v_ref))
    ]
    return list(zip(*loads))


def first_body(qkv_ref, send_ref, k_ref, v_ref, own_k_ref, own_v_ref, sems):
    place = my_place()
    pairs = start_pairs(place, qkv_ref, 1 - place[1], k_ref, v_ref, sems.at[0])
    later = start_pairs(place, qkv_ref, place[1], own_k_ref, own_v_ref, sems.at[1])
    each = send_ref.shape[0] // len(pairs)
    for i, pair in enumerate(pairs):
        for copy in pair:
            copy.wait()
        for h in range(i * each, (i + 1) * each):
            send_ref[h] = head_state(k_ref, v_ref, h).astype(BF16)
    for pair in later:
        for copy in pair:
            copy.wait()


def own_body(k_ref, v_ref, own_ref, low_ref):
    for h in range(own_ref.shape[0]):
        state = head_state(k_ref, v_ref, h)
        own_ref[h] = state
        low_ref[h] = state.astype(BF16)


def chip_body(own_ref, got_ref, *chip_refs):
    few = chip_refs[0].shape[0]
    for i, chip_ref in enumerate(chip_refs):
        for h in range(few):
            at = i * few + h
            chip_ref[h] = (own_ref[at] + got_ref[at].astype(F32)).astype(BF16)


def inside_body(qkv_ref, *refs):
    place = my_place()
    kv_refs = refs[:4]
    got_ref, gain_ref, inside_ref, q_ref, order_ref, scores_ref, sems = refs[4:]
    rows, width = kv_refs[0].shape
    loads = [
        start_loads(qkv_ref, 0, place, side, q_ref.at[i], sems.at[i])
        for i, side in enumerate((place[1], 1 - place[1]))
    ]
    allowed = lax.broadcasted_iota(jnp.int32, (rows, rows), 1) <= lax.broadcasted_iota(
        jnp.int32, (rows, rows), 0
    )
    each = width // DH // len(ORDER)
    for side in range(2):
        for i in range(len(ORDER)):
            loads[side][i].wait()
            for h in range(i * each, (i + 1) * each):
                cols = head_cols(h)
                scores = lax.dot_general(
                    q_ref[side, :, cols],
                    kv_refs[2 * side][:, cols],
                    (((1,), (1,)), ((), ())),
                    preferred_element_type=F32,
                )
                scores_ref[side, :, cols] = jnp.where(allowed, scores, 0.0).astype(BF16)
    for i, side in enumerate((place[1], 1 - place[1])):
        block = each * DH
        for j, d in enumerate(ORDER):
            start = (side * len(ORDER) + group_of(place, d, len(ORDER))) * block
            order_ref[i, :, pl.ds(j * block, block)] = gain_ref[:, columns(start, block)]

    def plain(side):
        for h in range(width // DH):
            cols = head_cols(h)
            inside_ref[side, :, cols] = jnp.dot(
                scores_ref[side, :, cols],
                kv_refs[2 * side + 1][:, cols],
                preferred_element_type=F32,
            )

    plain(1)

    @pl.when(place[1] == 0)
    def _():
        plain(0)

    @pl.when(place[1] != 0)
    def _():
        for h in range(width // DH):
            cols = head_cols(h)
            inside_ref[0, :, cols] = jnp.dot(
                jnp.concatenate([scores_ref[0, :, cols], q_ref[0, :, cols]], axis=1),
                jnp.concatenate([kv_refs[1][:, cols], got_ref[h]], axis=0),
                preferred_element_type=F32,
            )


def totals_body(*refs):
    chips, outs = refs[:-LINE], refs[-LINE:]
    _, _, m = line_place()
    few = outs[0].shape[0]
    for d, out in enumerate(outs):
        first = quarter_of(m, d) * few
        for h in range(few):
            out[h] = sum(c[first + h].astype(F32) for c in chips).astype(BF16)


def line_sum_body(*refs):
    out = refs[-1]
    few = refs[0].shape[0]
    for c in range(out.shape[0] // few):
        terms = refs[c * LINE : (c + 1) * LINE]
        for h in range(few):
            out[c * few + h] = sum(t[h].astype(F32) for t in terms).astype(BF16)


def line_priors_body(ny, mirror_ref, *refs):
    y, late, m = line_place()
    rows, refs = refs[: ny - 1], refs[ny - 1 :]
    n = len(refs) // 2
    terms, outs = refs[:n], refs[n:]
    few = outs[0].shape[0]
    seen = [jnp.where(y >= d, 1.0, 0.0) for d in range(1, ny)]
    turn = jnp.where(late, 1.0, 0.0)
    at = [jnp.where(late, -1, 1) * lax.rem(m - d + LINE, LINE) for d in range(LINE)]
    weight = [[jnp.where(at[e] < at[d], 1.0, 0.0) for e in range(LINE)] for d in range(LINE)]
    for c in range(n // LINE):
        for h in range(few):
            base = mirror_ref[c * few + h].astype(F32) * turn
            for r, row in enumerate(rows):
                base = base + row[c * few + h].astype(F32) * seen[r]
            values = [t[h].astype(F32) for t in terms[c * LINE : (c + 1) * LINE]]
            for d in range(LINE):
                acc = base
                for e in range(LINE):
                    if e != d:
                        acc = acc + values[e] * weight[d][e]
                outs[c * LINE + d][h] = acc.astype(BF16)


def chip_priors_body(*refs):
    place = my_place()
    _, _, m = line_place()
    bases, refs = refs[:LINE], refs[LINE:]
    n = len(refs) // 2
    chips, outs = refs[:n], refs[n:]
    few = bases[0].shape[0]
    for x in range(n):

        @pl.when(place[0] == x)
        def _():
            for d in range(LINE):
                first = quarter_of(m, d) * few
                for h in range(few):
                    acc = bases[d][h].astype(F32)
                    for chip in range(n):
                        i = ORDER.index((x - chip) % n)
                        outs[i][first + h] = acc.astype(BF16)
                        if chip < n - 1:
                            acc = acc + chips[i][first + h].astype(F32)


def give_body(starts, *refs):
    place = my_place()
    priors, low_ref, out_ref = refs[:-2], refs[-2], refs[-1]
    few = priors[0].shape[0]

    @pl.when(place[1] == 0)
    def _():
        for i, (prior_ref, start) in enumerate(zip(priors, starts)):
            for h in range(few):
                state = low_ref[start + h].astype(F32)
                out_ref[i * few + h] = (prior_ref[h].astype(F32) + state).astype(BF16)

    @pl.when(place[1] != 0)
    def _():
        for i, prior_ref in enumerate(priors):
            out_ref[i * few : (i + 1) * few] = prior_ref[...]


def attend(side, q_ref, inside_ref, gain_ref, heads, priors, out_ref, total):
    for at, (head, which, row) in enumerate(heads):
        cols = head_cols(head)
        value = jnp.dot(q_ref[side, :, cols], priors[which][row], preferred_element_type=F32)
        value = (inside_ref[side, :, cols] + value).astype(BF16).astype(F32)
        out_ref[:, head_cols(at)] = value * gain_ref[side, :, cols]
        total = total + value * value
    return total


def attend_body(sides, q_ref, inside_ref, gain_ref, *refs):
    n = len(sides)
    outs, sq_ref = refs[-1 - n : -1], refs[-1]
    total = jnp.zeros(sq_ref.shape, F32)
    for (side, first, count, heads), out_ref in zip(sides, outs):
        priors = refs[first : first + count]
        total = attend(side, q_ref, inside_ref, gain_ref, heads, priors, out_ref, total)
    sq_ref[...] = total


def finish_body(heads, sources, few, q_ref, inside_ref, gain_ref, *refs):
    place = my_place()
    n = len(ORDER)
    each = q_ref.shape[2] // DH // n
    out_ref, other, done, sems = refs[-4:]
    count = len(sources) - 1
    kept, sqs, priors = refs[:count], refs[count : count + CHUNKS], refs[count + CHUNKS : -4]
    total = sqs[0][...]
    for sq_ref in sqs[1:]:
        total = total + sq_ref[...]
    total = attend(1, q_ref, inside_ref, gain_ref, heads, priors, other, total)
    meansq = jnp.sum(total, axis=-1, keepdims=True) / out_ref.shape[1]
    scale = jnp.broadcast_to(lax.rsqrt(meansq + 1e-06), total.shape)
    copies = []
    for (side, chunk), source in zip(sources, (*kept, other)):
        for i, d in enumerate(ORDER):
            slot = len(copies)
            for h in range(few):
                value = source[:, head_cols(i * few + h)]
                done[slot, :, head_cols(h)] = (value * scale).astype(BF16)
            base = (place[1] if side == 0 else 1 - place[1]) * n
            first = (base + group_of(place, d, n)) * each + chunk * few
            copy = pltpu.make_async_copy(
                done.at[slot], out_ref.at[:, columns(first * DH, few * DH)], sems.at[slot]
            )
            copy.start()
            copies.append(copy)
    for copy in copies:
        copy.wait()


def per_device(nx, nctx, qkv, gain):
    rows, _, width = qkv.shape
    heads = width // DH
    half = heads // 2
    each = half // nx
    block = each * DH
    gain = gain.reshape(1, width)
    qkv = pltpu.with_memory_space_constraint(jnp.transpose(qkv, (1, 0, 2)), pltpu.HBM)
    swap = [(i, i ^ 1) for i in range(2 * nx)]

    def shift(d):
        return [(2 * x + c, 2 * ((x + d) % nx) + c) for x in range(nx) for c in range(2)]

    def states(n, dtype=BF16):
        return jax.ShapeDtypeStruct((n, DH, DH), dtype)

    def call(body, in_specs, out_specs, out_shape, products, nbytes, scratch=()):
        return pl.pallas_call(
            body,
            in_specs=in_specs,
            out_specs=out_specs,
            out_shape=out_shape,
            scratch_shapes=scratch,
            cost_estimate=pl.CostEstimate(
                flops=2 * products * rows * DH * DH, bytes_accessed=nbytes, transcendentals=0
            ),
            compiler_params=pltpu.CompilerParams(vmem_limit_bytes=16 * 2**20),
        )

    mib = 2**20
    matrix = jax.ShapeDtypeStruct((rows, width // 2), BF16)
    loads = pltpu.SemaphoreType.DMA((2, nx))
    send, keys, value_rows, own_keys, own_values = call(
        first_body,
        [HBM],
        [VMEM] * 5,
        [states(half)] + [matrix] * 4,
        half,
        5 * mib,
        scratch=[pltpu.SemaphoreType.DMA((2, 2, nx))],
    )(qkv)
    got = lax.ppermute(send, "tp", swap)
    own, low = call(
        own_body, [VMEM] * 2, [VMEM] * 2, [states(half, F32), states(half)], half, 5 * mib
    )(own_keys, own_values)
    few = each // CHUNKS
    ny = nctx // NZ
    made = call(
        chip_body,
        [VMEM, VMEM],
        [VMEM] * (nx * CHUNKS),
        [states(few)] * (nx * CHUNKS),
        0,
        4 * mib,
    )(own, got)
    chips = [[made[i * CHUNKS + c] for i in range(nx)] for c in range(CHUNKS)]
    if CHUNKS == 1:
        gain, chips[-1][-1] = lax.optimization_barrier((gain, chips[-1][-1]))
    chips = [
        [t if d == 0 else lax.ppermute(t, "tp", shift(d)) for d, t in zip(ORDER, chunk)]
        for chunk in chips
    ]
    wide = (2, rows, width // 2)

    def local(gain):
        return call(
            inside_body,
            [HBM] + [VMEM] * 6,
            [VMEM] * 3,
            [
                jax.ShapeDtypeStruct(wide, F32),
                jax.ShapeDtypeStruct(wide, BF16),
                jax.ShapeDtypeStruct((2, 1, width // 2), F32),
            ],
            4 * half,
            12 * mib,
            scratch=[pltpu.VMEM(wide, BF16), loads],
        )(qkv, own_keys, own_values, keys, value_rows, got, gain)

    if CHUNKS == 1:
        inside, queries, gains = local(gain)
        inside, queries, gains, *chips[0] = lax.optimization_barrier(
            (inside, queries, gains, *chips[0])
        )

    def pos(late, m):
        return NZ - 1 - m if late else m

    def line(d):
        return [
            (y * NZ + pos(late, m), y * NZ + pos(late, (m + d) % LINE))
            for y in range(ny)
            for late in range(2)
            for m in range(LINE)
        ]

    mirror = [(y * NZ + z, y * NZ + NZ - 1 - z) for y in range(ny) for z in range(NZ)]

    def row(d):
        return [(y * NZ + z, (y + d) % ny * NZ + z) for y in range(ny) for z in range(NZ)]

    small = few // LINE
    terms = []
    for chunk in chips:
        totals = call(
            totals_body, [VMEM] * nx, [VMEM] * LINE, [states(small)] * LINE, 0, mib
        )(*chunk)
        terms += [
            t if d == 0 else lax.ppermute(t, "ctx", line(d)) for d, t in enumerate(totals)
        ]
    held = CHUNKS * small
    mine = call(line_sum_body, [VMEM] * len(terms), VMEM, states(held), 0, mib)(*terms)
    facing = lax.ppermute(mine, "ctx", mirror)
    whole = (mine.astype(F32) + facing.astype(F32)).astype(BF16)
    rows_before = [lax.ppermute(whole, "ctx", row(d)) for d in range(1, ny)]
    bases = call(
        functools.partial(line_priors_body, ny),
        [VMEM] * (ny + len(terms)),
        [VMEM] * len(terms),
        [states(small)] * len(terms),
        0,
        mib,
    )(facing, *rows_before, *terms)
    bases = [
        b if k % LINE == 0 else lax.ppermute(b, "ctx", line(-(k % LINE)))
        for k, b in enumerate(bases)
    ]
    parts = []
    for c in range(CHUNKS):
        made = call(
            chip_priors_body,
            [VMEM] * (LINE + nx),
            [VMEM] * nx,
            [states(few)] * nx,
            0,
            2 * mib,
        )(*bases[c * LINE : (c + 1) * LINE], *chips[c])
        if CHUNKS > 1 and c == CHUNKS - 1:
            made = list(made)
            gain, made[-1] = lax.optimization_barrier((gain, made[-1]))
            inside, queries, gains = local(gain)
        parts.append(
            [p if d == 0 else lax.ppermute(p, "tp", shift(-d)) for d, p in zip(ORDER, made)]
        )

    def give(c, which):
        given = call(
            functools.partial(give_body, [(i * CHUNKS + c) * few for i in which]),
            [VMEM] * (len(which) + 1),
            VMEM,
            states(few * len(which)),
            0,
            mib,
        )(*[parts[c][i] for i in which], low)
        return lax.ppermute(given, "tp", swap)

    kept, sqs, sources = [], [], []
    square = jax.ShapeDtypeStruct((rows, DH), F32)
    for c in range(CHUNKS):
        last = c == CHUNKS - 1
        groups = [[i] for i in range(nx)] if last else [list(range(nx))]
        others = [give(c, g) for g in groups]
        own_heads = [
            (i * each + c * few + h, i, h) for i in range(nx) for h in range(few)
        ]
        other_heads = [
            (i * each + c * few + h, g, k * few + h)
            for g, group in enumerate(groups)
            for k, i in enumerate(group)
            for h in range(few)
        ]
        sides = [(0, 0, nx, own_heads)]
        if not last:
            sides.append((1, nx, len(others), other_heads))
        sources += [(side[0], c) for side in sides]
        priors = parts[c] + ([] if last else others)
        out = jax.ShapeDtypeStruct((rows, nx * few * DH), F32)
        *outs, sq = call(
            functools.partial(attend_body, sides),
            [VMEM] * (3 + len(priors)),
            [VMEM] * (len(sides) + 1),
            [out] * len(sides) + [square],
            half,
            5 * mib,
        )(queries, inside, gains, *priors)
        kept += outs
        sqs.append(sq)
    sources.append((1, CHUNKS - 1))
    return call(
        functools.partial(finish_body, other_heads, sources, few),
        [VMEM] * (3 + len(kept) + len(sqs) + len(others)),
        HBM,
        jax.ShapeDtypeStruct((rows, width), BF16),
        half,
        7 * mib,
        scratch=[
            pltpu.VMEM((rows, nx * few * DH), F32),
            pltpu.VMEM((2 * nx * CHUNKS, rows, few * DH), BF16),
            pltpu.SemaphoreType.DMA((2 * nx * CHUNKS,)),
        ],
    )(queries, inside, gains, *kept, *sqs, *others)


def solution(mesh):
    return jax.shard_map(
        functools.partial(per_device, mesh.shape["tp"] // 2, mesh.shape["ctx"]),
        mesh=mesh,
        in_specs=(P(("ctx", "tp"), None, None), P()),
        out_specs=P(("ctx", "tp"), None),
        check_vma=False,
    )
```

```python
import functools

import jax
import jax.numpy as jnp
from jax import lax
from jax.experimental import pallas as pl
from jax.experimental.pallas import tpu as pltpu
from jax.sharding import PartitionSpec as P

DH = 128
F32 = jnp.float32
BF16 = jnp.bfloat16
VMEM = pl.BlockSpec(memory_space=pltpu.VMEM)
HBM = pl.BlockSpec(memory_space=pltpu.HBM)


ORDER = (2, 1, 3, 0)
CHUNKS = 1
NZ = 8
LINE = NZ // 2
FACING = 6


def my_place():
    tp = lax.axis_index("tp")
    return tp // 2, lax.rem(tp, 2)


def line_place():
    ctx = lax.axis_index("ctx")
    z = lax.rem(ctx, NZ)
    late = z >= LINE
    return ctx // NZ, late, jnp.where(late, z ^ FACING, z)


def quarter_of(m, d):
    return m ^ d


def group_of(place, d, n):
    return place[0] ^ d


def columns(start, size):
    return pl.ds(pl.multiple_of(start, size), size)


def head_cols(h):
    return pl.ds(h * DH, DH)


def head_state(k_ref, v_ref, h):
    cols = head_cols(h)
    return lax.dot_general(
        k_ref[:, cols], v_ref[:, cols], (((0,), (0,)), ((), ())), preferred_element_type=F32
    )


def start_loads(qkv_ref, which, place, side, buf, sems):
    block = buf.shape[1] // len(ORDER)
    copies = []
    for i, d in enumerate(ORDER):
        start = (side * len(ORDER) + group_of(place, d, len(ORDER))) * block
        copy = pltpu.make_async_copy(
            qkv_ref.at[which, :, columns(start, block)],
            buf.at[:, pl.ds(i * block, block)],
            sems.at[i],
        )
        copy.start()
        copies.append(copy)
    return copies


def start_pairs(place, qkv_ref, side, k_ref, v_ref, sems):
    loads = [
        start_loads(qkv_ref, 1 + i, place, side, buf, sems.at[i])
        for i, buf in enumerate((k_ref, v_ref))
    ]
    return list(zip(*loads))


def first_body(qkv_ref, send_ref, k_ref, v_ref, own_k_ref, own_v_ref, sems):
    place = my_place()
    pairs = start_pairs(place, qkv_ref, 1 - place[1], k_ref, v_ref, sems.at[0])
    later = start_pairs(place, qkv_ref, place[1], own_k_ref, own_v_ref, sems.at[1])
    each = send_ref.shape[0] // len(pairs)
    for i, pair in enumerate(pairs):
        for copy in pair:
            copy.wait()
        for h in range(i * each, (i + 1) * each):
            send_ref[h] = head_state(k_ref, v_ref, h).astype(BF16)
    for pair in later:
        for copy in pair:
            copy.wait()


def own_body(k_ref, v_ref, own_ref, low_ref):
    for h in range(own_ref.shape[0]):
        state = head_state(k_ref, v_ref, h)
        own_ref[h] = state
        low_ref[h] = state.astype(BF16)


def chip_body(own_ref, got_ref, *chip_refs):
    few = chip_refs[0].shape[0]
    for i, chip_ref in enumerate(chip_refs):
        for h in range(few):
            at = i * few + h
            chip_ref[h] = (own_ref[at] + got_ref[at].astype(F32)).astype(BF16)


def inside_body(qkv_ref, *refs):
    place = my_place()
    kv_refs = refs[:4]
    got_ref, gain_ref, inside_ref, q_ref, order_ref, scores_ref, sems = refs[4:]
    rows, width = kv_refs[0].shape
    loads = [
        start_loads(qkv_ref, 0, place, side, q_ref.at[i], sems.at[i])
        for i, side in enumerate((place[1], 1 - place[1]))
    ]
    allowed = lax.broadcasted_iota(jnp.int32, (rows, rows), 1) <= lax.broadcasted_iota(
        jnp.int32, (rows, rows), 0
    )
    each = width // DH // len(ORDER)
    for side in range(2):
        for i in range(len(ORDER)):
            loads[side][i].wait()
            for h in range(i * each, (i + 1) * each):
                cols = head_cols(h)
                scores = lax.dot_general(
                    q_ref[side, :, cols],
                    kv_refs[2 * side][:, cols],
                    (((1,), (1,)), ((), ())),
                    preferred_element_type=F32,
                )
                scores_ref[side, :, cols] = jnp.where(allowed, scores, 0.0).astype(BF16)
    for i, side in enumerate((place[1], 1 - place[1])):
        block = each * DH
        for j, d in enumerate(ORDER):
            start = (side * len(ORDER) + group_of(place, d, len(ORDER))) * block
            order_ref[i, :, pl.ds(j * block, block)] = gain_ref[:, columns(start, block)]

    def plain(side):
        for h in range(width // DH):
            cols = head_cols(h)
            inside_ref[side, :, cols] = jnp.dot(
                scores_ref[side, :, cols],
                kv_refs[2 * side + 1][:, cols],
                preferred_element_type=F32,
            )

    plain(1)

    @pl.when(place[1] == 0)
    def _():
        plain(0)

    @pl.when(place[1] != 0)
    def _():
        for h in range(width // DH):
            cols = head_cols(h)
            inside_ref[0, :, cols] = jnp.dot(
                jnp.concatenate([scores_ref[0, :, cols], q_ref[0, :, cols]], axis=1),
                jnp.concatenate([kv_refs[1][:, cols], got_ref[h]], axis=0),
                preferred_element_type=F32,
            )


def totals_body(*refs):
    chips, outs = refs[:-LINE], refs[-LINE:]
    _, _, m = line_place()
    few = outs[0].shape[0]
    for d, out in enumerate(outs):
        first = quarter_of(m, d) * few
        for h in range(few):
            out[h] = sum(c[first + h].astype(F32) for c in chips).astype(BF16)


def line_sum_body(*refs):
    out = refs[-1]
    few = refs[0].shape[0]
    for c in range(out.shape[0] // few):
        terms = refs[c * LINE : (c + 1) * LINE]
        for h in range(few):
            out[c * few + h] = sum(t[h].astype(F32) for t in terms).astype(BF16)


def line_priors_body(ny, mirror_ref, *refs):
    y, late, m = line_place()
    rows, refs = refs[: ny - 1], refs[ny - 1 :]
    n = len(refs) // 2
    terms, outs = refs[:n], refs[n:]
    few = outs[0].shape[0]
    seen = [jnp.where(y > y ^ d, 1.0, 0.0) for d in range(1, ny)]
    turn = jnp.where(late, 1.0, 0.0)
    turned = jnp.where(late, FACING % LINE, 0)
    at = [m ^ d ^ turned for d in range(LINE)]
    weight = [[jnp.where(at[e] < at[d], 1.0, 0.0) for e in range(LINE)] for d in range(LINE)]
    for c in range(n // LINE):
        for h in range(few):
            base = mirror_ref[c * few + h].astype(F32) * turn
            for r, row in enumerate(rows):
                base = base + row[c * few + h].astype(F32) * seen[r]
            values = [t[h].astype(F32) for t in terms[c * LINE : (c + 1) * LINE]]
            for d in range(LINE):
                acc = base
                for e in range(LINE):
                    if e != d:
                        acc = acc + values[e] * weight[d][e]
                outs[c * LINE + d][h] = acc.astype(BF16)


def chip_priors_body(*refs):
    place = my_place()
    _, _, m = line_place()
    bases, refs = refs[:LINE], refs[LINE:]
    n = len(refs) // 2
    chips, outs = refs[:n], refs[n:]
    few = bases[0].shape[0]
    for x in range(n):

        @pl.when(place[0] == x)
        def _():
            for d in range(LINE):
                first = quarter_of(m, d) * few
                for h in range(few):
                    acc = bases[d][h].astype(F32)
                    for chip in range(n):
                        i = ORDER.index(x ^ chip)
                        outs[i][first + h] = acc.astype(BF16)
                        if chip < n - 1:
                            acc = acc + chips[i][first + h].astype(F32)


def give_body(starts, *refs):
    place = my_place()
    priors, low_ref, out_ref = refs[:-2], refs[-2], refs[-1]
    few = priors[0].shape[0]

    @pl.when(place[1] == 0)
    def _():
        for i, (prior_ref, start) in enumerate(zip(priors, starts)):
            for h in range(few):
                state = low_ref[start + h].astype(F32)
                out_ref[i * few + h] = (prior_ref[h].astype(F32) + state).astype(BF16)

    @pl.when(place[1] != 0)
    def _():
        for i, prior_ref in enumerate(priors):
            out_ref[i * few : (i + 1) * few] = prior_ref[...]


def attend(side, q_ref, inside_ref, gain_ref, heads, priors, out_ref, total):
    for at, (head, which, row) in enumerate(heads):
        cols = head_cols(head)
        value = jnp.dot(q_ref[side, :, cols], priors[which][row], preferred_element_type=F32)
        value = (inside_ref[side, :, cols] + value).astype(BF16).astype(F32)
        out_ref[:, head_cols(at)] = value * gain_ref[side, :, cols]
        total = total + value * value
    return total


def attend_body(sides, q_ref, inside_ref, gain_ref, *refs):
    n = len(sides)
    outs, sq_ref = refs[-1 - n : -1], refs[-1]
    total = jnp.zeros(sq_ref.shape, F32)
    for (side, first, count, heads), out_ref in zip(sides, outs):
        priors = refs[first : first + count]
        total = attend(side, q_ref, inside_ref, gain_ref, heads, priors, out_ref, total)
    sq_ref[...] = total


def finish_body(heads, sources, few, q_ref, inside_ref, gain_ref, *refs):
    place = my_place()
    n = len(ORDER)
    each = q_ref.shape[2] // DH // n
    out_ref, other, done, sems = refs[-4:]
    count = len(sources) - 1
    kept, sqs, priors = refs[:count], refs[count : count + CHUNKS], refs[count + CHUNKS : -4]
    total = sqs[0][...]
    for sq_ref in sqs[1:]:
        total = total + sq_ref[...]
    total = attend(1, q_ref, inside_ref, gain_ref, heads, priors, other, total)
    meansq = jnp.sum(total, axis=-1, keepdims=True) / out_ref.shape[1]
    scale = jnp.broadcast_to(lax.rsqrt(meansq + 1e-06), total.shape)
    copies = []
    for (side, chunk), source in zip(sources, (*kept, other)):
        for i, d in enumerate(ORDER):
            slot = len(copies)
            for h in range(few):
                value = source[:, head_cols(i * few + h)]
                done[slot, :, head_cols(h)] = (value * scale).astype(BF16)
            base = (place[1] if side == 0 else 1 - place[1]) * n
            first = (base + group_of(place, d, n)) * each + chunk * few
            copy = pltpu.make_async_copy(
                done.at[slot], out_ref.at[:, columns(first * DH, few * DH)], sems.at[slot]
            )
            copy.start()
            copies.append(copy)
    for copy in copies:
        copy.wait()


def per_device(nx, nctx, qkv, gain):
    rows, _, width = qkv.shape
    heads = width // DH
    half = heads // 2
    each = half // nx
    block = each * DH
    gain = gain.reshape(1, width)
    qkv = pltpu.with_memory_space_constraint(jnp.transpose(qkv, (1, 0, 2)), pltpu.HBM)
    swap = [(i, i ^ 1) for i in range(2 * nx)]

    def shift(d):
        return [(2 * x + c, 2 * (x ^ d) + c) for x in range(nx) for c in range(2)]

    def states(n, dtype=BF16):
        return jax.ShapeDtypeStruct((n, DH, DH), dtype)

    def call(body, in_specs, out_specs, out_shape, products, nbytes, scratch=()):
        return pl.pallas_call(
            body,
            in_specs=in_specs,
            out_specs=out_specs,
            out_shape=out_shape,
            scratch_shapes=scratch,
            cost_estimate=pl.CostEstimate(
                flops=2 * products * rows * DH * DH, bytes_accessed=nbytes, transcendentals=0
            ),
            compiler_params=pltpu.CompilerParams(vmem_limit_bytes=16 * 2**20),
        )

    mib = 2**20
    matrix = jax.ShapeDtypeStruct((rows, width // 2), BF16)
    loads = pltpu.SemaphoreType.DMA((2, nx))
    send, keys, value_rows, own_keys, own_values = call(
        first_body,
        [HBM],
        [VMEM] * 5,
        [states(half)] + [matrix] * 4,
        half,
        5 * mib,
        scratch=[pltpu.SemaphoreType.DMA((2, 2, nx))],
    )(qkv)
    got = lax.ppermute(send, "tp", swap)
    own, low = call(
        own_body, [VMEM] * 2, [VMEM] * 2, [states(half, F32), states(half)], half, 5 * mib
    )(own_keys, own_values)
    few = each // CHUNKS
    ny = nctx // NZ
    made = call(
        chip_body,
        [VMEM, VMEM],
        [VMEM] * (nx * CHUNKS),
        [states(few)] * (nx * CHUNKS),
        0,
        4 * mib,
    )(own, got)
    chips = [[made[i * CHUNKS + c] for i in range(nx)] for c in range(CHUNKS)]
    if CHUNKS == 1:
        gain, chips[-1][-1] = lax.optimization_barrier((gain, chips[-1][-1]))
    chips = [
        [t if d == 0 else lax.ppermute(t, "tp", shift(d)) for d, t in zip(ORDER, chunk)]
        for chunk in chips
    ]
    wide = (2, rows, width // 2)

    def local(gain):
        return call(
            inside_body,
            [HBM] + [VMEM] * 6,
            [VMEM] * 3,
            [
                jax.ShapeDtypeStruct(wide, F32),
                jax.ShapeDtypeStruct(wide, BF16),
                jax.ShapeDtypeStruct((2, 1, width // 2), F32),
            ],
            4 * half,
            12 * mib,
            scratch=[pltpu.VMEM(wide, BF16), loads],
        )(qkv, own_keys, own_values, keys, value_rows, got, gain)

    if CHUNKS == 1:
        inside, queries, gains = local(gain)
        inside, queries, gains, *chips[0] = lax.optimization_barrier(
            (inside, queries, gains, *chips[0])
        )

    def pos(late, m):
        return m ^ FACING if late else m

    def line(d):
        return [
            (y * NZ + pos(late, m), y * NZ + pos(late, m ^ d))
            for y in range(ny)
            for late in range(2)
            for m in range(LINE)
        ]

    mirror = [(y * NZ + z, y * NZ + (z ^ FACING)) for y in range(ny) for z in range(NZ)]

    def row(d):
        return [(y * NZ + z, (y ^ d) * NZ + z) for y in range(ny) for z in range(NZ)]

    small = few // LINE
    terms = []
    for chunk in chips:
        totals = call(
            totals_body, [VMEM] * nx, [VMEM] * LINE, [states(small)] * LINE, 0, mib
        )(*chunk)
        terms += [
            t if d == 0 else lax.ppermute(t, "ctx", line(d)) for d, t in enumerate(totals)
        ]
    held = CHUNKS * small
    mine = call(line_sum_body, [VMEM] * len(terms), VMEM, states(held), 0, mib)(*terms)
    facing = lax.ppermute(mine, "ctx", mirror)
    whole = (mine.astype(F32) + facing.astype(F32)).astype(BF16)
    rows_before = [lax.ppermute(whole, "ctx", row(d)) for d in range(1, ny)]
    bases = call(
        functools.partial(line_priors_body, ny),
        [VMEM] * (ny + len(terms)),
        [VMEM] * len(terms),
        [states(small)] * len(terms),
        0,
        mib,
    )(facing, *rows_before, *terms)
    bases = [
        b if k % LINE == 0 else lax.ppermute(b, "ctx", line(k % LINE))
        for k, b in enumerate(bases)
    ]
    parts = []
    for c in range(CHUNKS):
        made = call(
            chip_priors_body,
            [VMEM] * (LINE + nx),
            [VMEM] * nx,
            [states(few)] * nx,
            0,
            2 * mib,
        )(*bases[c * LINE : (c + 1) * LINE], *chips[c])
        if CHUNKS > 1 and c == CHUNKS - 1:
            made = list(made)
            gain, made[-1] = lax.optimization_barrier((gain, made[-1]))
            inside, queries, gains = local(gain)
        parts.append(
            [p if d == 0 else lax.ppermute(p, "tp", shift(d)) for d, p in zip(ORDER, made)]
        )

    def give(c, which):
        given = call(
            functools.partial(give_body, [(i * CHUNKS + c) * few for i in which]),
            [VMEM] * (len(which) + 1),
            VMEM,
            states(few * len(which)),
            0,
            mib,
        )(*[parts[c][i] for i in which], low)
        return lax.ppermute(given, "tp", swap)

    kept, sqs, sources = [], [], []
    square = jax.ShapeDtypeStruct((rows, DH), F32)
    for c in range(CHUNKS):
        last = c == CHUNKS - 1
        groups = [[i] for i in range(nx)] if last else [list(range(nx))]
        others = [give(c, g) for g in groups]
        own_heads = [
            (i * each + c * few + h, i, h) for i in range(nx) for h in range(few)
        ]
        other_heads = [
            (i * each + c * few + h, g, k * few + h)
            for g, group in enumerate(groups)
            for k, i in enumerate(group)
            for h in range(few)
        ]
        sides = [(0, 0, nx, own_heads)]
        if not last:
            sides.append((1, nx, len(others), other_heads))
        sources += [(side[0], c) for side in sides]
        priors = parts[c] + ([] if last else others)
        out = jax.ShapeDtypeStruct((rows, nx * few * DH), F32)
        *outs, sq = call(
            functools.partial(attend_body, sides),
            [VMEM] * (3 + len(priors)),
            [VMEM] * (len(sides) + 1),
            [out] * len(sides) + [square],
            half,
            5 * mib,
        )(queries, inside, gains, *priors)
        kept += outs
        sqs.append(sq)
    sources.append((1, CHUNKS - 1))
    return call(
        functools.partial(finish_body, other_heads, sources, few),
        [VMEM] * (3 + len(kept) + len(sqs) + len(others)),
        HBM,
        jax.ShapeDtypeStruct((rows, width), BF16),
        half,
        7 * mib,
        scratch=[
            pltpu.VMEM((rows, nx * few * DH), F32),
            pltpu.VMEM((2 * nx * CHUNKS, rows, few * DH), BF16),
            pltpu.SemaphoreType.DMA((2 * nx * CHUNKS,)),
        ],
    )(queries, inside, gains, *kept, *sqs, *others)


def solution(mesh):
    return jax.shard_map(
        functools.partial(per_device, mesh.shape["tp"] // 2, mesh.shape["ctx"]),
        mesh=mesh,
        in_specs=(P(("ctx", "tp"), None, None), P()),
        out_specs=P(("ctx", "tp"), None),
        check_vma=False,
    )
```

```python
import functools

import jax
import jax.numpy as jnp
from jax import lax
from jax.experimental import pallas as pl
from jax.experimental.pallas import tpu as pltpu
from jax.sharding import PartitionSpec as P

DH = 128
F32 = jnp.float32
BF16 = jnp.bfloat16
VMEM = pl.BlockSpec(memory_space=pltpu.VMEM)
HBM = pl.BlockSpec(memory_space=pltpu.HBM)


ORDER = (1, 3, 2, 0)
CHUNKS = 1
NZ = 8
LINE = NZ // 2
FACING = 6


def my_place():
    tp = lax.axis_index("tp")
    return tp // 2, lax.rem(tp, 2)


def line_place():
    ctx = lax.axis_index("ctx")
    z = lax.rem(ctx, NZ)
    late = z >= LINE
    return ctx // NZ, late, jnp.where(late, z ^ FACING, z)


def quarter_of(m, d):
    return m ^ d


def group_of(place, d, n):
    return place[0] ^ d


def columns(start, size):
    return pl.ds(pl.multiple_of(start, size), size)


def head_cols(h):
    return pl.ds(h * DH, DH)


def head_state(k_ref, v_ref, h):
    cols = head_cols(h)
    return lax.dot_general(
        k_ref[:, cols], v_ref[:, cols], (((0,), (0,)), ((), ())), preferred_element_type=F32
    )


def start_loads(qkv_ref, which, place, side, buf, sems):
    block = buf.shape[1] // len(ORDER)
    copies = []
    for i, d in enumerate(ORDER):
        start = (side * len(ORDER) + group_of(place, d, len(ORDER))) * block
        copy = pltpu.make_async_copy(
            qkv_ref.at[which, :, columns(start, block)],
            buf.at[:, pl.ds(i * block, block)],
            sems.at[i],
        )
        copy.start()
        copies.append(copy)
    return copies


def start_pairs(place, qkv_ref, side, k_ref, v_ref, sems):
    loads = [
        start_loads(qkv_ref, 1 + i, place, side, buf, sems.at[i])
        for i, buf in enumerate((k_ref, v_ref))
    ]
    return list(zip(*loads))


def first_body(qkv_ref, send0_ref, send1_ref, k_ref, v_ref, own_k_ref, own_v_ref, sems):
    place = my_place()
    pairs = start_pairs(place, qkv_ref, 1 - place[1], k_ref, v_ref, sems.at[0])
    later = start_pairs(place, qkv_ref, place[1], own_k_ref, own_v_ref, sems.at[1])
    few = send0_ref.shape[0]
    each = 2 * few // len(pairs)
    for i, pair in enumerate(pairs):
        for copy in pair:
            copy.wait()
        for h in range(i * each, (i + 1) * each):
            send_ref = send0_ref if h < few else send1_ref
            send_ref[h % few] = head_state(k_ref, v_ref, h).astype(BF16)
    for pair in later:
        for copy in pair:
            copy.wait()


def own_body(k_ref, v_ref, own_ref, low_ref):
    for h in range(own_ref.shape[0]):
        state = head_state(k_ref, v_ref, h)
        own_ref[h] = state
        low_ref[h] = state.astype(BF16)


def chip_body(before, own_ref, got_ref, *chip_refs):
    few = chip_refs[0].shape[0]
    for i, chip_ref in enumerate(chip_refs):
        for h in range(few):
            at = i * few + h
            chip_ref[h] = (own_ref[before + at] + got_ref[at].astype(F32)).astype(BF16)


def inside_body(qkv_ref, *refs):
    place = my_place()
    kv_refs = refs[:4]
    got_refs = refs[4:6]
    gain_ref, inside_ref, q_ref, order_ref, scores_ref, sems = refs[6:]
    few = got_refs[0].shape[0]
    rows, width = kv_refs[0].shape
    loads = [
        start_loads(qkv_ref, 0, place, side, q_ref.at[i], sems.at[i])
        for i, side in enumerate((place[1], 1 - place[1]))
    ]
    allowed = lax.broadcasted_iota(jnp.int32, (rows, rows), 1) <= lax.broadcasted_iota(
        jnp.int32, (rows, rows), 0
    )
    each = width // DH // len(ORDER)
    for side in range(2):
        for i in range(len(ORDER)):
            loads[side][i].wait()
            for h in range(i * each, (i + 1) * each):
                cols = head_cols(h)
                scores = lax.dot_general(
                    q_ref[side, :, cols],
                    kv_refs[2 * side][:, cols],
                    (((1,), (1,)), ((), ())),
                    preferred_element_type=F32,
                )
                scores_ref[side, :, cols] = jnp.where(allowed, scores, 0.0).astype(BF16)
    for i, side in enumerate((place[1], 1 - place[1])):
        block = each * DH
        for j, d in enumerate(ORDER):
            start = (side * len(ORDER) + group_of(place, d, len(ORDER))) * block
            order_ref[i, :, pl.ds(j * block, block)] = gain_ref[:, columns(start, block)]

    def plain(side):
        for h in range(width // DH):
            cols = head_cols(h)
            inside_ref[side, :, cols] = jnp.dot(
                scores_ref[side, :, cols],
                kv_refs[2 * side + 1][:, cols],
                preferred_element_type=F32,
            )

    plain(1)

    @pl.when(place[1] == 0)
    def _():
        plain(0)

    @pl.when(place[1] != 0)
    def _():
        for h in range(width // DH):
            cols = head_cols(h)
            inside_ref[0, :, cols] = jnp.dot(
                jnp.concatenate([scores_ref[0, :, cols], q_ref[0, :, cols]], axis=1),
                jnp.concatenate([kv_refs[1][:, cols], got_refs[h // few][h % few]], axis=0),
                preferred_element_type=F32,
            )


def totals_body(*refs):
    chips, outs = refs[:-LINE], refs[-LINE:]
    _, _, m = line_place()
    few = outs[0].shape[0]
    for d, out in enumerate(outs):
        first = quarter_of(m, d) * few
        for h in range(few):
            out[h] = sum(c[first + h].astype(F32) for c in chips).astype(BF16)


def line_sum_body(*refs):
    out = refs[-1]
    few = refs[0].shape[0]
    for c in range(out.shape[0] // few):
        terms = refs[c * LINE : (c + 1) * LINE]
        for h in range(few):
            out[c * few + h] = sum(t[h].astype(F32) for t in terms).astype(BF16)


def line_priors_body(ny, mirror_ref, *refs):
    y, late, m = line_place()
    rows, refs = refs[: ny - 1], refs[ny - 1 :]
    n = len(refs) // 2
    terms, outs = refs[:n], refs[n:]
    few = outs[0].shape[0]
    seen = [jnp.where(y > y ^ d, 1.0, 0.0) for d in range(1, ny)]
    turn = jnp.where(late, 1.0, 0.0)
    turned = jnp.where(late, FACING % LINE, 0)
    at = [m ^ d ^ turned for d in range(LINE)]
    weight = [[jnp.where(at[e] < at[d], 1.0, 0.0) for e in range(LINE)] for d in range(LINE)]
    for c in range(n // LINE):
        for h in range(few):
            base = mirror_ref[c * few + h].astype(F32) * turn
            for r, row in enumerate(rows):
                base = base + row[c * few + h].astype(F32) * seen[r]
            values = [t[h].astype(F32) for t in terms[c * LINE : (c + 1) * LINE]]
            for d in range(LINE):
                acc = base
                for e in range(LINE):
                    if e != d:
                        acc = acc + values[e] * weight[d][e]
                outs[c * LINE + d][h] = acc.astype(BF16)


def chip_priors_body(*refs):
    place = my_place()
    _, _, m = line_place()
    bases, refs = refs[:LINE], refs[LINE:]
    n = len(refs) // 2
    chips, outs = refs[:n], refs[n:]
    few = bases[0].shape[0]
    for x in range(n):

        @pl.when(place[0] == x)
        def _():
            for d in range(LINE):
                first = quarter_of(m, d) * few
                for h in range(few):
                    acc = bases[d][h].astype(F32)
                    for chip in range(n):
                        i = ORDER.index(x ^ chip)
                        outs[i][first + h] = acc.astype(BF16)
                        if chip < n - 1:
                            acc = acc + chips[i][first + h].astype(F32)


def give_body(starts, *refs):
    place = my_place()
    priors, low_ref, out_ref = refs[:-2], refs[-2], refs[-1]
    few = priors[0].shape[0]

    @pl.when(place[1] == 0)
    def _():
        for i, (prior_ref, start) in enumerate(zip(priors, starts)):
            for h in range(few):
                state = low_ref[start + h].astype(F32)
                out_ref[i * few + h] = (prior_ref[h].astype(F32) + state).astype(BF16)

    @pl.when(place[1] != 0)
    def _():
        for i, prior_ref in enumerate(priors):
            out_ref[i * few : (i + 1) * few] = prior_ref[...]


def attend(side, q_ref, inside_ref, gain_ref, heads, priors, out_ref, total):
    for at, (head, which, row) in enumerate(heads):
        cols = head_cols(head)
        value = jnp.dot(q_ref[side, :, cols], priors[which][row], preferred_element_type=F32)
        value = (inside_ref[side, :, cols] + value).astype(BF16).astype(F32)
        out_ref[:, head_cols(at)] = value * gain_ref[side, :, cols]
        total = total + value * value
    return total


def attend_body(sides, q_ref, inside_ref, gain_ref, *refs):
    n = len(sides)
    outs, sq_ref = refs[-1 - n : -1], refs[-1]
    total = jnp.zeros(sq_ref.shape, F32)
    for (side, first, count, heads), out_ref in zip(sides, outs):
        priors = refs[first : first + count]
        total = attend(side, q_ref, inside_ref, gain_ref, heads, priors, out_ref, total)
    sq_ref[...] = total


def finish_body(heads, sources, few, q_ref, inside_ref, gain_ref, *refs):
    place = my_place()
    n = len(ORDER)
    each = q_ref.shape[2] // DH // n
    out_ref, other, done, sems = refs[-4:]
    count = len(sources) - 1
    kept, sqs, priors = refs[:count], refs[count : count + CHUNKS], refs[count + CHUNKS : -4]
    total = sqs[0][...]
    for sq_ref in sqs[1:]:
        total = total + sq_ref[...]
    total = attend(1, q_ref, inside_ref, gain_ref, heads, priors, other, total)
    meansq = jnp.sum(total, axis=-1, keepdims=True) / out_ref.shape[1]
    scale = jnp.broadcast_to(lax.rsqrt(meansq + 1e-06), total.shape)
    copies = []
    for (side, chunk), source in zip(sources, (*kept, other)):
        for i, d in enumerate(ORDER):
            slot = len(copies)
            for h in range(few):
                value = source[:, head_cols(i * few + h)]
                done[slot, :, head_cols(h)] = (value * scale).astype(BF16)
            base = (place[1] if side == 0 else 1 - place[1]) * n
            first = (base + group_of(place, d, n)) * each + chunk * few
            copy = pltpu.make_async_copy(
                done.at[slot], out_ref.at[:, columns(first * DH, few * DH)], sems.at[slot]
            )
            copy.start()
            copies.append(copy)
    for copy in copies:
        copy.wait()


def per_device(nx, nctx, qkv, gain):
    rows, _, width = qkv.shape
    heads = width // DH
    half = heads // 2
    each = half // nx
    block = each * DH
    gain = gain.reshape(1, width)
    qkv = pltpu.with_memory_space_constraint(jnp.transpose(qkv, (1, 0, 2)), pltpu.HBM)
    swap = [(i, i ^ 1) for i in range(2 * nx)]

    def shift(d):
        return [(2 * x + c, 2 * (x ^ d) + c) for x in range(nx) for c in range(2)]

    def states(n, dtype=BF16):
        return jax.ShapeDtypeStruct((n, DH, DH), dtype)

    def call(body, in_specs, out_specs, out_shape, products, nbytes, scratch=()):
        return pl.pallas_call(
            body,
            in_specs=in_specs,
            out_specs=out_specs,
            out_shape=out_shape,
            scratch_shapes=scratch,
            cost_estimate=pl.CostEstimate(
                flops=2 * products * rows * DH * DH, bytes_accessed=nbytes, transcendentals=0
            ),
            compiler_params=pltpu.CompilerParams(vmem_limit_bytes=16 * 2**20),
        )

    mib = 2**20
    matrix = jax.ShapeDtypeStruct((rows, width // 2), BF16)
    loads = pltpu.SemaphoreType.DMA((2, nx))
    send0, send1, keys, value_rows, own_keys, own_values = call(
        first_body,
        [HBM],
        [VMEM] * 6,
        [states(half // 2)] * 2 + [matrix] * 4,
        half,
        5 * mib,
        scratch=[pltpu.SemaphoreType.DMA((2, 2, nx))],
    )(qkv)
    got = [lax.ppermute(send, "tp", swap) for send in (send0, send1)]
    own, low = call(
        own_body, [VMEM] * 2, [VMEM] * 2, [states(half, F32), states(half)], half, 5 * mib
    )(own_keys, own_values)
    few = each // CHUNKS
    ny = nctx // NZ
    made = []
    for i in range(2):
        made += call(
            functools.partial(chip_body, i * half // 2),
            [VMEM, VMEM],
            [VMEM] * (nx * CHUNKS // 2),
            [states(few)] * (nx * CHUNKS // 2),
            0,
            2 * mib,
        )(own, got[i])
    chips = [[made[i * CHUNKS + c] for i in range(nx)] for c in range(CHUNKS)]
    if CHUNKS == 1:
        gain, chips[-1][-1] = lax.optimization_barrier((gain, chips[-1][-1]))
    chips = [
        [t if d == 0 else lax.ppermute(t, "tp", shift(d)) for d, t in zip(ORDER, chunk)]
        for chunk in chips
    ]
    wide = (2, rows, width // 2)

    def local(gain):
        return call(
            inside_body,
            [HBM] + [VMEM] * 7,
            [VMEM] * 3,
            [
                jax.ShapeDtypeStruct(wide, F32),
                jax.ShapeDtypeStruct(wide, BF16),
                jax.ShapeDtypeStruct((2, 1, width // 2), F32),
            ],
            4 * half,
            12 * mib,
            scratch=[pltpu.VMEM(wide, BF16), loads],
        )(qkv, own_keys, own_values, keys, value_rows, *got, gain)

    if CHUNKS == 1:
        inside, queries, gains = local(gain)
        inside, queries, gains, *chips[0] = lax.optimization_barrier(
            (inside, queries, gains, *chips[0])
        )

    def pos(late, m):
        return m ^ FACING if late else m

    def line(d):
        return [
            (y * NZ + pos(late, m), y * NZ + pos(late, m ^ d))
            for y in range(ny)
            for late in range(2)
            for m in range(LINE)
        ]

    mirror = [(y * NZ + z, y * NZ + (z ^ FACING)) for y in range(ny) for z in range(NZ)]

    def row(d):
        return [(y * NZ + z, (y ^ d) * NZ + z) for y in range(ny) for z in range(NZ)]

    small = few // LINE
    terms = []
    for chunk in chips:
        totals = call(
            totals_body, [VMEM] * nx, [VMEM] * LINE, [states(small)] * LINE, 0, mib
        )(*chunk)
        terms += [
            t if d == 0 else lax.ppermute(t, "ctx", line(d)) for d, t in enumerate(totals)
        ]
    held = CHUNKS * small
    mine = call(line_sum_body, [VMEM] * len(terms), VMEM, states(held), 0, mib)(*terms)
    facing = lax.ppermute(mine, "ctx", mirror)
    whole = (mine.astype(F32) + facing.astype(F32)).astype(BF16)
    rows_before = [lax.ppermute(whole, "ctx", row(d)) for d in range(1, ny)]
    bases = call(
        functools.partial(line_priors_body, ny),
        [VMEM] * (ny + len(terms)),
        [VMEM] * len(terms),
        [states(small)] * len(terms),
        0,
        mib,
    )(facing, *rows_before, *terms)
    bases = [
        b if k % LINE == 0 else lax.ppermute(b, "ctx", line(k % LINE))
        for k, b in enumerate(bases)
    ]
    parts = []
    for c in range(CHUNKS):
        made = call(
            chip_priors_body,
            [VMEM] * (LINE + nx),
            [VMEM] * nx,
            [states(few)] * nx,
            0,
            2 * mib,
        )(*bases[c * LINE : (c + 1) * LINE], *chips[c])
        if CHUNKS > 1 and c == CHUNKS - 1:
            made = list(made)
            gain, made[-1] = lax.optimization_barrier((gain, made[-1]))
            inside, queries, gains = local(gain)
        parts.append(
            [p if d == 0 else lax.ppermute(p, "tp", shift(d)) for d, p in zip(ORDER, made)]
        )

    def give(c, which):
        given = call(
            functools.partial(give_body, [(i * CHUNKS + c) * few for i in which]),
            [VMEM] * (len(which) + 1),
            VMEM,
            states(few * len(which)),
            0,
            mib,
        )(*[parts[c][i] for i in which], low)
        return lax.ppermute(given, "tp", swap)

    kept, sqs, sources = [], [], []
    square = jax.ShapeDtypeStruct((rows, DH), F32)
    for c in range(CHUNKS):
        last = c == CHUNKS - 1
        groups = [[i] for i in range(nx)] if last else [list(range(nx))]
        others = [give(c, g) for g in groups]
        own_heads = [
            (i * each + c * few + h, i, h) for i in range(nx) for h in range(few)
        ]
        other_heads = [
            (i * each + c * few + h, g, k * few + h)
            for g, group in enumerate(groups)
            for k, i in enumerate(group)
            for h in range(few)
        ]
        sides = [(0, 0, nx, own_heads)]
        if not last:
            sides.append((1, nx, len(others), other_heads))
        sources += [(side[0], c) for side in sides]
        priors = parts[c] + ([] if last else others)
        out = jax.ShapeDtypeStruct((rows, nx * few * DH), F32)
        *outs, sq = call(
            functools.partial(attend_body, sides),
            [VMEM] * (3 + len(priors)),
            [VMEM] * (len(sides) + 1),
            [out] * len(sides) + [square],
            half,
            5 * mib,
        )(queries, inside, gains, *priors)
        kept += outs
        sqs.append(sq)
    sources.append((1, CHUNKS - 1))
    return call(
        functools.partial(finish_body, other_heads, sources, few),
        [VMEM] * (3 + len(kept) + len(sqs) + len(others)),
        HBM,
        jax.ShapeDtypeStruct((rows, width), BF16),
        half,
        7 * mib,
        scratch=[
            pltpu.VMEM((rows, nx * few * DH), F32),
            pltpu.VMEM((2 * nx * CHUNKS, rows, few * DH), BF16),
            pltpu.SemaphoreType.DMA((2 * nx * CHUNKS,)),
        ],
    )(queries, inside, gains, *kept, *sqs, *others)


def solution(mesh):
    return jax.shard_map(
        functools.partial(per_device, mesh.shape["tp"] // 2, mesh.shape["ctx"]),
        mesh=mesh,
        in_specs=(P(("ctx", "tp"), None, None), P()),
        out_specs=P(("ctx", "tp"), None),
        check_vma=False,
    )
```

```python
import functools

import jax
import jax.numpy as jnp
from jax import lax
from jax.experimental import pallas as pl
from jax.experimental.pallas import tpu as pltpu
from jax.sharding import PartitionSpec as P

DH = 128
F32 = jnp.float32
BF16 = jnp.bfloat16
VMEM = pl.BlockSpec(memory_space=pltpu.VMEM)
HBM = pl.BlockSpec(memory_space=pltpu.HBM)


ORDER = (1, 3, 2, 0)
CHUNKS = 1
BATCHES = 4
NZ = 8
LINE = NZ // 2
FACING = 6


def my_place():
    tp = lax.axis_index("tp")
    return tp // 2, lax.rem(tp, 2)


def line_place():
    ctx = lax.axis_index("ctx")
    z = lax.rem(ctx, NZ)
    late = z >= LINE
    return ctx // NZ, late, jnp.where(late, z ^ FACING, z)


def quarter_of(m, d):
    return m ^ d


def group_of(place, d, n):
    return place[0] ^ d


def columns(start, size):
    return pl.ds(pl.multiple_of(start, size), size)


def head_cols(h):
    return pl.ds(h * DH, DH)


def head_state(k_ref, v_ref, h):
    cols = head_cols(h)
    return lax.dot_general(
        k_ref[:, cols], v_ref[:, cols], (((0,), (0,)), ((), ())), preferred_element_type=F32
    )


def start_loads(qkv_ref, which, place, side, buf, sems):
    block = buf.shape[1] // len(ORDER)
    copies = []
    for i, d in enumerate(ORDER):
        start = (side * len(ORDER) + group_of(place, d, len(ORDER))) * block
        copy = pltpu.make_async_copy(
            qkv_ref.at[which, :, columns(start, block)],
            buf.at[:, pl.ds(i * block, block)],
            sems.at[i],
        )
        copy.start()
        copies.append(copy)
    return copies


def start_pairs(place, qkv_ref, side, k_ref, v_ref, sems):
    loads = [
        start_loads(qkv_ref, 1 + i, place, side, buf, sems.at[i])
        for i, buf in enumerate((k_ref, v_ref))
    ]
    return list(zip(*loads))


def first_body(qkv_ref, *refs):
    send_refs, (k_ref, v_ref, own_k_ref, own_v_ref, sems) = refs[:-5], refs[-5:]
    place = my_place()
    pairs = start_pairs(place, qkv_ref, 1 - place[1], k_ref, v_ref, sems.at[0])
    later = start_pairs(place, qkv_ref, place[1], own_k_ref, own_v_ref, sems.at[1])
    few = send_refs[0].shape[0]
    each = len(send_refs) * few // len(pairs)
    for i, pair in enumerate(pairs):
        for copy in pair:
            copy.wait()
        for h in range(i * each, (i + 1) * each):
            send_refs[h // few][h % few] = head_state(k_ref, v_ref, h).astype(BF16)
    for pair in later:
        for copy in pair:
            copy.wait()


def own_body(k_ref, v_ref, own_ref, low_ref):
    for h in range(own_ref.shape[0]):
        state = head_state(k_ref, v_ref, h)
        own_ref[h] = state
        low_ref[h] = state.astype(BF16)


def chip_body(before, own_ref, got_ref, *chip_refs):
    few = chip_refs[0].shape[0]
    for i, chip_ref in enumerate(chip_refs):
        for h in range(few):
            at = i * few + h
            chip_ref[h] = (own_ref[before + at] + got_ref[at].astype(F32)).astype(BF16)


def inside_body(qkv_ref, *refs):
    place = my_place()
    kv_refs = refs[:4]
    got_refs = refs[4:-6]
    gain_ref, inside_ref, q_ref, order_ref, scores_ref, sems = refs[-6:]
    few = got_refs[0].shape[0]
    rows, width = kv_refs[0].shape
    loads = [
        start_loads(qkv_ref, 0, place, side, q_ref.at[i], sems.at[i])
        for i, side in enumerate((place[1], 1 - place[1]))
    ]
    allowed = lax.broadcasted_iota(jnp.int32, (rows, rows), 1) <= lax.broadcasted_iota(
        jnp.int32, (rows, rows), 0
    )
    each = width // DH // len(ORDER)
    for side in range(2):
        for i in range(len(ORDER)):
            loads[side][i].wait()
            for h in range(i * each, (i + 1) * each):
                cols = head_cols(h)
                scores = lax.dot_general(
                    q_ref[side, :, cols],
                    kv_refs[2 * side][:, cols],
                    (((1,), (1,)), ((), ())),
                    preferred_element_type=F32,
                )
                scores_ref[side, :, cols] = jnp.where(allowed, scores, 0.0).astype(BF16)
    for i, side in enumerate((place[1], 1 - place[1])):
        block = each * DH
        for j, d in enumerate(ORDER):
            start = (side * len(ORDER) + group_of(place, d, len(ORDER))) * block
            order_ref[i, :, pl.ds(j * block, block)] = gain_ref[:, columns(start, block)]

    def plain(side):
        for h in range(width // DH):
            cols = head_cols(h)
            inside_ref[side, :, cols] = jnp.dot(
                scores_ref[side, :, cols],
                kv_refs[2 * side + 1][:, cols],
                preferred_element_type=F32,
            )

    plain(1)

    @pl.when(place[1] == 0)
    def _():
        plain(0)

    @pl.when(place[1] != 0)
    def _():
        for h in range(width // DH):
            cols = head_cols(h)
            inside_ref[0, :, cols] = jnp.dot(
                jnp.concatenate([scores_ref[0, :, cols], q_ref[0, :, cols]], axis=1),
                jnp.concatenate([kv_refs[1][:, cols], got_refs[h // few][h % few]], axis=0),
                preferred_element_type=F32,
            )


def totals_body(*refs):
    chips, outs = refs[:-LINE], refs[-LINE:]
    _, _, m = line_place()
    few = outs[0].shape[0]
    for d, out in enumerate(outs):
        first = quarter_of(m, d) * few
        for h in range(few):
            out[h] = sum(c[first + h].astype(F32) for c in chips).astype(BF16)


def line_sum_body(*refs):
    out = refs[-1]
    few = refs[0].shape[0]
    for c in range(out.shape[0] // few):
        terms = refs[c * LINE : (c + 1) * LINE]
        for h in range(few):
            out[c * few + h] = sum(t[h].astype(F32) for t in terms).astype(BF16)


def line_priors_body(ny, mirror_ref, *refs):
    y, late, m = line_place()
    rows, refs = refs[: ny - 1], refs[ny - 1 :]
    n = len(refs) // 2
    terms, outs = refs[:n], refs[n:]
    few = outs[0].shape[0]
    seen = [jnp.where(y > y ^ d, 1.0, 0.0) for d in range(1, ny)]
    turn = jnp.where(late, 1.0, 0.0)
    turned = jnp.where(late, FACING % LINE, 0)
    at = [m ^ d ^ turned for d in range(LINE)]
    weight = [[jnp.where(at[e] < at[d], 1.0, 0.0) for e in range(LINE)] for d in range(LINE)]
    for c in range(n // LINE):
        for h in range(few):
            base = mirror_ref[c * few + h].astype(F32) * turn
            for r, row in enumerate(rows):
                base = base + row[c * few + h].astype(F32) * seen[r]
            values = [t[h].astype(F32) for t in terms[c * LINE : (c + 1) * LINE]]
            for d in range(LINE):
                acc = base
                for e in range(LINE):
                    if e != d:
                        acc = acc + values[e] * weight[d][e]
                outs[c * LINE + d][h] = acc.astype(BF16)


def chip_priors_body(*refs):
    place = my_place()
    _, _, m = line_place()
    bases, refs = refs[:LINE], refs[LINE:]
    n = len(refs) // 2
    chips, outs = refs[:n], refs[n:]
    few = bases[0].shape[0]
    for x in range(n):

        @pl.when(place[0] == x)
        def _():
            for d in range(LINE):
                first = quarter_of(m, d) * few
                for h in range(few):
                    acc = bases[d][h].astype(F32)
                    for chip in range(n):
                        i = ORDER.index(x ^ chip)
                        outs[i][first + h] = acc.astype(BF16)
                        if chip < n - 1:
                            acc = acc + chips[i][first + h].astype(F32)


def give_body(starts, *refs):
    place = my_place()
    priors, low_ref, out_ref = refs[:-2], refs[-2], refs[-1]
    few = priors[0].shape[0]

    @pl.when(place[1] == 0)
    def _():
        for i, (prior_ref, start) in enumerate(zip(priors, starts)):
            for h in range(few):
                state = low_ref[start + h].astype(F32)
                out_ref[i * few + h] = (prior_ref[h].astype(F32) + state).astype(BF16)

    @pl.when(place[1] != 0)
    def _():
        for i, prior_ref in enumerate(priors):
            out_ref[i * few : (i + 1) * few] = prior_ref[...]


def attend(side, q_ref, inside_ref, gain_ref, heads, priors, out_ref, total):
    for at, (head, which, row) in enumerate(heads):
        cols = head_cols(head)
        value = jnp.dot(q_ref[side, :, cols], priors[which][row], preferred_element_type=F32)
        value = (inside_ref[side, :, cols] + value).astype(BF16).astype(F32)
        out_ref[:, head_cols(at)] = value * gain_ref[side, :, cols]
        total = total + value * value
    return total


def attend_body(sides, q_ref, inside_ref, gain_ref, *refs):
    n = len(sides)
    outs, sq_ref = refs[-1 - n : -1], refs[-1]
    total = jnp.zeros(sq_ref.shape, F32)
    for (side, first, count, heads), out_ref in zip(sides, outs):
        priors = refs[first : first + count]
        total = attend(side, q_ref, inside_ref, gain_ref, heads, priors, out_ref, total)
    sq_ref[...] = total


def finish_body(heads, sources, few, q_ref, inside_ref, gain_ref, *refs):
    place = my_place()
    n = len(ORDER)
    each = q_ref.shape[2] // DH // n
    out_ref, other, done, sems = refs[-4:]
    count = len(sources) - 1
    kept, sqs, priors = refs[:count], refs[count : count + CHUNKS], refs[count + CHUNKS : -4]
    total = sqs[0][...]
    for sq_ref in sqs[1:]:
        total = total + sq_ref[...]
    total = attend(1, q_ref, inside_ref, gain_ref, heads, priors, other, total)
    meansq = jnp.sum(total, axis=-1, keepdims=True) / out_ref.shape[1]
    scale = jnp.broadcast_to(lax.rsqrt(meansq + 1e-06), total.shape)
    copies = []
    for (side, chunk), source in zip(sources, (*kept, other)):
        for i, d in enumerate(ORDER):
            slot = len(copies)
            for h in range(few):
                value = source[:, head_cols(i * few + h)]
                done[slot, :, head_cols(h)] = (value * scale).astype(BF16)
            base = (place[1] if side == 0 else 1 - place[1]) * n
            first = (base + group_of(place, d, n)) * each + chunk * few
            copy = pltpu.make_async_copy(
                done.at[slot], out_ref.at[:, columns(first * DH, few * DH)], sems.at[slot]
            )
            copy.start()
            copies.append(copy)
    for copy in copies:
        copy.wait()


def per_device(nx, nctx, qkv, gain):
    rows, _, width = qkv.shape
    heads = width // DH
    half = heads // 2
    each = half // nx
    block = each * DH
    gain = gain.reshape(1, width)
    qkv = pltpu.with_memory_space_constraint(jnp.transpose(qkv, (1, 0, 2)), pltpu.HBM)
    swap = [(i, i ^ 1) for i in range(2 * nx)]

    def shift(d):
        return [(2 * x + c, 2 * (x ^ d) + c) for x in range(nx) for c in range(2)]

    def states(n, dtype=BF16):
        return jax.ShapeDtypeStruct((n, DH, DH), dtype)

    def call(body, in_specs, out_specs, out_shape, products, nbytes, scratch=()):
        return pl.pallas_call(
            body,
            in_specs=in_specs,
            out_specs=out_specs,
            out_shape=out_shape,
            scratch_shapes=scratch,
            cost_estimate=pl.CostEstimate(
                flops=2 * products * rows * DH * DH, bytes_accessed=nbytes, transcendentals=0
            ),
            compiler_params=pltpu.CompilerParams(vmem_limit_bytes=16 * 2**20),
        )

    mib = 2**20
    matrix = jax.ShapeDtypeStruct((rows, width // 2), BF16)
    loads = pltpu.SemaphoreType.DMA((2, nx))
    *sends, keys, value_rows, own_keys, own_values = call(
        first_body,
        [HBM],
        [VMEM] * (BATCHES + 4),
        [states(half // BATCHES)] * BATCHES + [matrix] * 4,
        half,
        5 * mib,
        scratch=[pltpu.SemaphoreType.DMA((2, 2, nx))],
    )(qkv)
    got = [lax.ppermute(send, "tp", swap) for send in sends]
    own, low = call(
        own_body, [VMEM] * 2, [VMEM] * 2, [states(half, F32), states(half)], half, 5 * mib
    )(own_keys, own_values)
    few = each // CHUNKS
    ny = nctx // NZ
    made = []
    for i in range(BATCHES):
        made += call(
            functools.partial(chip_body, i * half // BATCHES),
            [VMEM, VMEM],
            [VMEM] * (nx * CHUNKS // BATCHES),
            [states(few)] * (nx * CHUNKS // BATCHES),
            0,
            2 * mib,
        )(own, got[i])
    chips = [[made[i * CHUNKS + c] for i in range(nx)] for c in range(CHUNKS)]
    if CHUNKS == 1:
        gain, chips[-1][-1] = lax.optimization_barrier((gain, chips[-1][-1]))
    chips = [
        [t if d == 0 else lax.ppermute(t, "tp", shift(d)) for d, t in zip(ORDER, chunk)]
        for chunk in chips
    ]
    wide = (2, rows, width // 2)

    def local(gain):
        return call(
            inside_body,
            [HBM] + [VMEM] * (5 + BATCHES),
            [VMEM] * 3,
            [
                jax.ShapeDtypeStruct(wide, F32),
                jax.ShapeDtypeStruct(wide, BF16),
                jax.ShapeDtypeStruct((2, 1, width // 2), F32),
            ],
            4 * half,
            12 * mib,
            scratch=[pltpu.VMEM(wide, BF16), loads],
        )(qkv, own_keys, own_values, keys, value_rows, *got, gain)

    if CHUNKS == 1:
        inside, queries, gains = local(gain)
        inside, queries, gains, *chips[0] = lax.optimization_barrier(
            (inside, queries, gains, *chips[0])
        )

    def pos(late, m):
        return m ^ FACING if late else m

    def line(d):
        return [
            (y * NZ + pos(late, m), y * NZ + pos(late, m ^ d))
            for y in range(ny)
            for late in range(2)
            for m in range(LINE)
        ]

    mirror = [(y * NZ + z, y * NZ + (z ^ FACING)) for y in range(ny) for z in range(NZ)]

    def row(d):
        return [(y * NZ + z, (y ^ d) * NZ + z) for y in range(ny) for z in range(NZ)]

    small = few // LINE
    terms = []
    for chunk in chips:
        totals = call(
            totals_body, [VMEM] * nx, [VMEM] * LINE, [states(small)] * LINE, 0, mib
        )(*chunk)
        terms += [
            t if d == 0 else lax.ppermute(t, "ctx", line(d)) for d, t in enumerate(totals)
        ]
    held = CHUNKS * small
    mine = call(line_sum_body, [VMEM] * len(terms), VMEM, states(held), 0, mib)(*terms)
    facing = lax.ppermute(mine, "ctx", mirror)
    whole = (mine.astype(F32) + facing.astype(F32)).astype(BF16)
    rows_before = [lax.ppermute(whole, "ctx", row(d)) for d in range(1, ny)]
    bases = call(
        functools.partial(line_priors_body, ny),
        [VMEM] * (ny + len(terms)),
        [VMEM] * len(terms),
        [states(small)] * len(terms),
        0,
        mib,
    )(facing, *rows_before, *terms)
    bases = [
        b if k % LINE == 0 else lax.ppermute(b, "ctx", line(k % LINE))
        for k, b in enumerate(bases)
    ]
    parts = []
    for c in range(CHUNKS):
        made = call(
            chip_priors_body,
            [VMEM] * (LINE + nx),
            [VMEM] * nx,
            [states(few)] * nx,
            0,
            2 * mib,
        )(*bases[c * LINE : (c + 1) * LINE], *chips[c])
        if CHUNKS > 1 and c == CHUNKS - 1:
            made = list(made)
            gain, made[-1] = lax.optimization_barrier((gain, made[-1]))
            inside, queries, gains = local(gain)
        parts.append(
            [p if d == 0 else lax.ppermute(p, "tp", shift(d)) for d, p in zip(ORDER, made)]
        )

    def give(c, which):
        given = call(
            functools.partial(give_body, [(i * CHUNKS + c) * few for i in which]),
            [VMEM] * (len(which) + 1),
            VMEM,
            states(few * len(which)),
            0,
            mib,
        )(*[parts[c][i] for i in which], low)
        return lax.ppermute(given, "tp", swap)

    kept, sqs, sources = [], [], []
    square = jax.ShapeDtypeStruct((rows, DH), F32)
    for c in range(CHUNKS):
        last = c == CHUNKS - 1
        groups = [[i] for i in range(nx)] if last else [list(range(nx))]
        others = [give(c, g) for g in groups]
        own_heads = [
            (i * each + c * few + h, i, h) for i in range(nx) for h in range(few)
        ]
        other_heads = [
            (i * each + c * few + h, g, k * few + h)
            for g, group in enumerate(groups)
            for k, i in enumerate(group)
            for h in range(few)
        ]
        sides = [(0, 0, nx, own_heads)]
        if not last:
            sides.append((1, nx, len(others), other_heads))
        sources += [(side[0], c) for side in sides]
        priors = parts[c] + ([] if last else others)
        out = jax.ShapeDtypeStruct((rows, nx * few * DH), F32)
        *outs, sq = call(
            functools.partial(attend_body, sides),
            [VMEM] * (3 + len(priors)),
            [VMEM] * (len(sides) + 1),
            [out] * len(sides) + [square],
            half,
            5 * mib,
        )(queries, inside, gains, *priors)
        kept += outs
        sqs.append(sq)
    sources.append((1, CHUNKS - 1))
    return call(
        functools.partial(finish_body, other_heads, sources, few),
        [VMEM] * (3 + len(kept) + len(sqs) + len(others)),
        HBM,
        jax.ShapeDtypeStruct((rows, width), BF16),
        half,
        7 * mib,
        scratch=[
            pltpu.VMEM((rows, nx * few * DH), F32),
            pltpu.VMEM((2 * nx * CHUNKS, rows, few * DH), BF16),
            pltpu.SemaphoreType.DMA((2 * nx * CHUNKS,)),
        ],
    )(queries, inside, gains, *kept, *sqs, *others)


def solution(mesh):
    return jax.shard_map(
        functools.partial(per_device, mesh.shape["tp"] // 2, mesh.shape["ctx"]),
        mesh=mesh,
        in_specs=(P(("ctx", "tp"), None, None), P()),
        out_specs=P(("ctx", "tp"), None),
        check_vma=False,
    )
```

```python
import functools

import jax
import jax.numpy as jnp
from jax import lax
from jax.experimental import pallas as pl
from jax.experimental.pallas import tpu as pltpu
from jax.sharding import PartitionSpec as P

DH = 128
F32 = jnp.float32
BF16 = jnp.bfloat16
VMEM = pl.BlockSpec(memory_space=pltpu.VMEM)
HBM = pl.BlockSpec(memory_space=pltpu.HBM)


ORDER = (1, 3, 2, 0)
CHUNKS = 1
NZ = 8
LINE = NZ // 2
FACING = 6


def my_place():
    tp = lax.axis_index("tp")
    return tp // 2, lax.rem(tp, 2)


def line_place():
    ctx = lax.axis_index("ctx")
    z = lax.rem(ctx, NZ)
    late = z >= LINE
    return ctx // NZ, late, jnp.where(late, z ^ FACING, z)


def quarter_of(m, d):
    return m ^ d


def group_of(place, d, n):
    return place[0] ^ d


def columns(start, size):
    return pl.ds(pl.multiple_of(start, size), size)


def head_cols(h):
    return pl.ds(h * DH, DH)


def head_state(k_ref, v_ref, h):
    cols = head_cols(h)
    return lax.dot_general(
        k_ref[:, cols], v_ref[:, cols], (((0,), (0,)), ((), ())), preferred_element_type=F32
    )


def start_loads(qkv_ref, which, place, side, buf, sems):
    block = buf.shape[1] // len(ORDER)
    copies = []
    for i, d in enumerate(ORDER):
        start = (side * len(ORDER) + group_of(place, d, len(ORDER))) * block
        copy = pltpu.make_async_copy(
            qkv_ref.at[which, :, columns(start, block)],
            buf.at[:, pl.ds(i * block, block)],
            sems.at[i],
        )
        copy.start()
        copies.append(copy)
    return copies


def start_pairs(place, qkv_ref, side, k_ref, v_ref, sems):
    loads = [
        start_loads(qkv_ref, 1 + i, place, side, buf, sems.at[i])
        for i, buf in enumerate((k_ref, v_ref))
    ]
    return list(zip(*loads))


def first_body(qkv_ref, send0_ref, send1_ref, k_ref, v_ref, own_k_ref, own_v_ref, sems):
    place = my_place()
    pairs = start_pairs(place, qkv_ref, 1 - place[1], k_ref, v_ref, sems.at[0])
    later = start_pairs(place, qkv_ref, place[1], own_k_ref, own_v_ref, sems.at[1])
    few = send0_ref.shape[0]
    each = 2 * few // len(pairs)
    for i, pair in enumerate(pairs):
        for copy in pair:
            copy.wait()
        for h in range(i * each, (i + 1) * each):
            send_ref = send0_ref if h < few else send1_ref
            send_ref[h % few] = head_state(k_ref, v_ref, h).astype(BF16)
    for pair in later:
        for copy in pair:
            copy.wait()


def own_body(k_ref, v_ref, own_ref, low_ref):
    for h in range(own_ref.shape[0]):
        state = head_state(k_ref, v_ref, h)
        own_ref[h] = state
        low_ref[h] = state.astype(BF16)


def chip_body(before, own_ref, got_ref, *chip_refs):
    few = chip_refs[0].shape[0]
    for i, chip_ref in enumerate(chip_refs):
        for h in range(few):
            at = i * few + h
            chip_ref[h] = (own_ref[before + at] + got_ref[at].astype(F32)).astype(BF16)


def inside_body(qkv_ref, *refs):
    place = my_place()
    kv_refs = refs[:4]
    got_refs = refs[4:6]
    gain_ref, inside_ref, q_ref, order_ref, scores_ref, sems = refs[6:]
    few = got_refs[0].shape[0]
    rows, width = kv_refs[0].shape
    loads = [
        start_loads(qkv_ref, 0, place, side, q_ref.at[i], sems.at[i])
        for i, side in enumerate((place[1], 1 - place[1]))
    ]
    allowed = lax.broadcasted_iota(jnp.int32, (rows, rows), 1) <= lax.broadcasted_iota(
        jnp.int32, (rows, rows), 0
    )
    each = width // DH // len(ORDER)
    for side in range(2):
        for i in range(len(ORDER)):
            loads[side][i].wait()
            for h in range(i * each, (i + 1) * each):
                cols = head_cols(h)
                scores = lax.dot_general(
                    q_ref[side, :, cols],
                    kv_refs[2 * side][:, cols],
                    (((1,), (1,)), ((), ())),
                    preferred_element_type=F32,
                )
                scores_ref[side, :, cols] = jnp.where(allowed, scores, 0.0).astype(BF16)
    for i, side in enumerate((place[1], 1 - place[1])):
        block = each * DH
        for j, d in enumerate(ORDER):
            start = (side * len(ORDER) + group_of(place, d, len(ORDER))) * block
            order_ref[i, :, pl.ds(j * block, block)] = gain_ref[:, columns(start, block)]

    def plain(side):
        for h in range(width // DH):
            cols = head_cols(h)
            inside_ref[side, :, cols] = jnp.dot(
                scores_ref[side, :, cols],
                kv_refs[2 * side + 1][:, cols],
                preferred_element_type=F32,
            )

    plain(1)

    @pl.when(place[1] == 0)
    def _():
        plain(0)

    @pl.when(place[1] != 0)
    def _():
        for h in range(width // DH):
            cols = head_cols(h)
            inside_ref[0, :, cols] = jnp.dot(
                jnp.concatenate([scores_ref[0, :, cols], q_ref[0, :, cols]], axis=1),
                jnp.concatenate([kv_refs[1][:, cols], got_refs[h // few][h % few]], axis=0),
                preferred_element_type=F32,
            )


def totals_body(*refs):
    chips, outs = refs[:-LINE], refs[-LINE:]
    _, _, m = line_place()
    few = outs[0].shape[0]
    for d, out in enumerate(outs):
        first = quarter_of(m, d) * few
        for h in range(few):
            out[h] = sum(c[first + h].astype(F32) for c in chips).astype(BF16)


def line_sum_body(*refs):
    out = refs[-1]
    few = refs[0].shape[0]
    for c in range(out.shape[0] // few):
        terms = refs[c * LINE : (c + 1) * LINE]
        for h in range(few):
            out[c * few + h] = sum(t[h].astype(F32) for t in terms).astype(BF16)


def line_priors_body(ny, mirror_ref, *refs):
    y, late, m = line_place()
    rows, refs = refs[: ny - 1], refs[ny - 1 :]
    n = len(refs) // 2
    terms, outs = refs[:n], refs[n:]
    few = outs[0].shape[0]
    seen = [jnp.where(y > y ^ d, 1.0, 0.0) for d in range(1, ny)]
    turn = jnp.where(late, 1.0, 0.0)
    turned = jnp.where(late, FACING % LINE, 0)
    at = [m ^ d ^ turned for d in range(LINE)]
    weight = [[jnp.where(at[e] < at[d], 1.0, 0.0) for e in range(LINE)] for d in range(LINE)]
    for c in range(n // LINE):
        for h in range(few):
            base = mirror_ref[c * few + h].astype(F32) * turn
            for r, row in enumerate(rows):
                base = base + row[c * few + h].astype(F32) * seen[r]
            values = [t[h].astype(F32) for t in terms[c * LINE : (c + 1) * LINE]]
            for d in range(LINE):
                acc = base
                for e in range(LINE):
                    if e != d:
                        acc = acc + values[e] * weight[d][e]
                outs[c * LINE + d][h] = acc.astype(BF16)


def chip_priors_body(*refs):
    place = my_place()
    _, _, m = line_place()
    bases, refs = refs[:LINE], refs[LINE:]
    n = len(refs) // 2
    chips, outs = refs[:n], refs[n:]
    few = bases[0].shape[0]
    for x in range(n):

        @pl.when(place[0] == x)
        def _():
            for d in range(LINE):
                first = quarter_of(m, d) * few
                for h in range(few):
                    acc = bases[d][h].astype(F32)
                    for chip in range(n):
                        i = ORDER.index(x ^ chip)
                        outs[i][first + h] = acc.astype(BF16)
                        if chip < n - 1:
                            acc = acc + chips[i][first + h].astype(F32)


def give_body(starts, *refs):
    place = my_place()
    priors, low_ref, out_ref = refs[:-2], refs[-2], refs[-1]
    few = priors[0].shape[0]

    @pl.when(place[1] == 0)
    def _():
        for i, (prior_ref, start) in enumerate(zip(priors, starts)):
            for h in range(few):
                state = low_ref[start + h].astype(F32)
                out_ref[i * few + h] = (prior_ref[h].astype(F32) + state).astype(BF16)

    @pl.when(place[1] != 0)
    def _():
        for i, prior_ref in enumerate(priors):
            out_ref[i * few : (i + 1) * few] = prior_ref[...]


def attend(side, q_ref, inside_ref, gain_ref, heads, priors, out_ref, total):
    for at, (head, which, row) in enumerate(heads):
        cols = head_cols(head)
        value = jnp.dot(q_ref[side, :, cols], priors[which][row], preferred_element_type=F32)
        value = (inside_ref[side, :, cols] + value).astype(BF16).astype(F32)
        out_ref[:, head_cols(at)] = value * gain_ref[side, :, cols]
        total = total + value * value
    return total


def attend_body(sides, q_ref, inside_ref, gain_ref, *refs):
    n = len(sides)
    outs, sq_ref = refs[-1 - n : -1], refs[-1]
    total = jnp.zeros(sq_ref.shape, F32)
    for (side, first, count, heads), out_ref in zip(sides, outs):
        priors = refs[first : first + count]
        total = attend(side, q_ref, inside_ref, gain_ref, heads, priors, out_ref, total)
    sq_ref[...] = total


def finish_body(heads, sources, few, q_ref, inside_ref, gain_ref, *refs):
    place = my_place()
    n = len(ORDER)
    each = q_ref.shape[2] // DH // n
    out_ref, other, done, sems = refs[-4:]
    count = len(sources) - 1
    kept, sqs, priors = refs[:count], refs[count : count + CHUNKS], refs[count + CHUNKS : -4]
    total = sqs[0][...]
    for sq_ref in sqs[1:]:
        total = total + sq_ref[...]
    total = attend(1, q_ref, inside_ref, gain_ref, heads, priors, other, total)
    meansq = jnp.sum(total, axis=-1, keepdims=True) / out_ref.shape[1]
    scale = jnp.broadcast_to(lax.rsqrt(meansq + 1e-06), total.shape)
    copies = []
    for (side, chunk, blocks), source in zip(sources, (*kept, other)):
        for i, block in enumerate(blocks):
            d = ORDER[block]
            slot = len(copies)
            for h in range(few):
                value = source[:, head_cols(i * few + h)]
                done[slot, :, head_cols(h)] = (value * scale).astype(BF16)
            base = (place[1] if side == 0 else 1 - place[1]) * n
            first = (base + group_of(place, d, n)) * each + chunk * few
            copy = pltpu.make_async_copy(
                done.at[slot], out_ref.at[:, columns(first * DH, few * DH)], sems.at[slot]
            )
            copy.start()
            copies.append(copy)
    for copy in copies:
        copy.wait()


def per_device(nx, nctx, qkv, gain):
    rows, _, width = qkv.shape
    heads = width // DH
    half = heads // 2
    each = half // nx
    block = each * DH
    gain = gain.reshape(1, width)
    qkv = pltpu.with_memory_space_constraint(jnp.transpose(qkv, (1, 0, 2)), pltpu.HBM)
    swap = [(i, i ^ 1) for i in range(2 * nx)]

    def shift(d):
        return [(2 * x + c, 2 * (x ^ d) + c) for x in range(nx) for c in range(2)]

    def states(n, dtype=BF16):
        return jax.ShapeDtypeStruct((n, DH, DH), dtype)

    def call(body, in_specs, out_specs, out_shape, products, nbytes, scratch=()):
        return pl.pallas_call(
            body,
            in_specs=in_specs,
            out_specs=out_specs,
            out_shape=out_shape,
            scratch_shapes=scratch,
            cost_estimate=pl.CostEstimate(
                flops=2 * products * rows * DH * DH, bytes_accessed=nbytes, transcendentals=0
            ),
            compiler_params=pltpu.CompilerParams(vmem_limit_bytes=16 * 2**20),
        )

    mib = 2**20
    matrix = jax.ShapeDtypeStruct((rows, width // 2), BF16)
    loads = pltpu.SemaphoreType.DMA((2, nx))
    send0, send1, keys, value_rows, own_keys, own_values = call(
        first_body,
        [HBM],
        [VMEM] * 6,
        [states(half // 2)] * 2 + [matrix] * 4,
        half,
        5 * mib,
        scratch=[pltpu.SemaphoreType.DMA((2, 2, nx))],
    )(qkv)
    got = [lax.ppermute(send, "tp", swap) for send in (send0, send1)]
    own, low = call(
        own_body, [VMEM] * 2, [VMEM] * 2, [states(half, F32), states(half)], half, 5 * mib
    )(own_keys, own_values)
    few = each // CHUNKS
    ny = nctx // NZ
    made = []
    for i in range(2):
        made += call(
            functools.partial(chip_body, i * half // 2),
            [VMEM, VMEM],
            [VMEM] * (nx * CHUNKS // 2),
            [states(few)] * (nx * CHUNKS // 2),
            0,
            2 * mib,
        )(own, got[i])
    chips = [[made[i * CHUNKS + c] for i in range(nx)] for c in range(CHUNKS)]
    if CHUNKS == 1:
        gain, chips[-1][-1] = lax.optimization_barrier((gain, chips[-1][-1]))
    chips = [
        [t if d == 0 else lax.ppermute(t, "tp", shift(d)) for d, t in zip(ORDER, chunk)]
        for chunk in chips
    ]
    wide = (2, rows, width // 2)

    def local(gain):
        return call(
            inside_body,
            [HBM] + [VMEM] * 7,
            [VMEM] * 3,
            [
                jax.ShapeDtypeStruct(wide, F32),
                jax.ShapeDtypeStruct(wide, BF16),
                jax.ShapeDtypeStruct((2, 1, width // 2), F32),
            ],
            4 * half,
            12 * mib,
            scratch=[pltpu.VMEM(wide, BF16), loads],
        )(qkv, own_keys, own_values, keys, value_rows, *got, gain)

    if CHUNKS == 1:
        inside, queries, gains = local(gain)
        inside, queries, gains, *chips[0] = lax.optimization_barrier(
            (inside, queries, gains, *chips[0])
        )

    def pos(late, m):
        return m ^ FACING if late else m

    def line(d):
        return [
            (y * NZ + pos(late, m), y * NZ + pos(late, m ^ d))
            for y in range(ny)
            for late in range(2)
            for m in range(LINE)
        ]

    mirror = [(y * NZ + z, y * NZ + (z ^ FACING)) for y in range(ny) for z in range(NZ)]

    def row(d):
        return [(y * NZ + z, (y ^ d) * NZ + z) for y in range(ny) for z in range(NZ)]

    small = few // LINE
    terms = []
    for chunk in chips:
        totals = call(
            totals_body, [VMEM] * nx, [VMEM] * LINE, [states(small)] * LINE, 0, mib
        )(*chunk)
        terms += [
            t if d == 0 else lax.ppermute(t, "ctx", line(d)) for d, t in enumerate(totals)
        ]
    held = CHUNKS * small
    mine = call(line_sum_body, [VMEM] * len(terms), VMEM, states(held), 0, mib)(*terms)
    facing = lax.ppermute(mine, "ctx", mirror)
    whole = (mine.astype(F32) + facing.astype(F32)).astype(BF16)
    rows_before = [lax.ppermute(whole, "ctx", row(d)) for d in range(1, ny)]
    bases = call(
        functools.partial(line_priors_body, ny),
        [VMEM] * (ny + len(terms)),
        [VMEM] * len(terms),
        [states(small)] * len(terms),
        0,
        mib,
    )(facing, *rows_before, *terms)
    bases = [
        b if k % LINE == 0 else lax.ppermute(b, "ctx", line(k % LINE))
        for k, b in enumerate(bases)
    ]
    parts = []
    for c in range(CHUNKS):
        made = call(
            chip_priors_body,
            [VMEM] * (LINE + nx),
            [VMEM] * nx,
            [states(few)] * nx,
            0,
            2 * mib,
        )(*bases[c * LINE : (c + 1) * LINE], *chips[c])
        if CHUNKS > 1 and c == CHUNKS - 1:
            made = list(made)
            gain, made[-1] = lax.optimization_barrier((gain, made[-1]))
            inside, queries, gains = local(gain)
        parts.append(
            [p if d == 0 else lax.ppermute(p, "tp", shift(d)) for d, p in zip(ORDER, made)]
        )

    def give(c, which):
        given = call(
            functools.partial(give_body, [(i * CHUNKS + c) * few for i in which]),
            [VMEM] * (len(which) + 1),
            VMEM,
            states(few * len(which)),
            0,
            mib,
        )(*[parts[c][i] for i in which], low)
        return lax.ppermute(given, "tp", swap)

    kept, sqs, sources = [], [], []
    square = jax.ShapeDtypeStruct((rows, DH), F32)
    for c in range(CHUNKS):
        last = c == CHUNKS - 1
        groups = [[i] for i in range(nx)] if last else [list(range(nx))]
        others = [give(c, g) for g in groups]
        own_heads = [
            (i * each + c * few + h, i, h) for i in range(nx) for h in range(few)
        ]
        soon, late = [0, nx - 1], list(range(1, nx - 1))
        other_heads = [
            [(i * each + c * few + h, g, h) for g, i in enumerate(which) for h in range(few)]
            for which in (soon, late)
        ]
        sides = [(0, 0, nx, own_heads), (1, nx, len(soon), other_heads[0])]
        sources += [(0, c, list(range(nx))), (1, c, soon)]
        priors = parts[c] + [others[i] for i in soon]
        outs = [
            jax.ShapeDtypeStruct((rows, len(heads) * DH), F32) for _, _, _, heads in sides
        ]
        *outs, sq = call(
            functools.partial(attend_body, sides),
            [VMEM] * (3 + len(priors)),
            [VMEM] * (len(sides) + 1),
            outs + [square],
            half,
            5 * mib,
        )(queries, inside, gains, *priors)
        kept += outs
        sqs.append(sq)
    sources.append((1, CHUNKS - 1, late))
    others = [others[i] for i in late]
    return call(
        functools.partial(finish_body, other_heads[1], sources, few),
        [VMEM] * (3 + len(kept) + len(sqs) + len(others)),
        HBM,
        jax.ShapeDtypeStruct((rows, width), BF16),
        half,
        7 * mib,
        scratch=[
            pltpu.VMEM((rows, len(late) * few * DH), F32),
            pltpu.VMEM((2 * nx * CHUNKS, rows, few * DH), BF16),
            pltpu.SemaphoreType.DMA((2 * nx * CHUNKS,)),
        ],
    )(queries, inside, gains, *kept, *sqs, *others)


def solution(mesh):
    return jax.shard_map(
        functools.partial(per_device, mesh.shape["tp"] // 2, mesh.shape["ctx"]),
        mesh=mesh,
        in_specs=(P(("ctx", "tp"), None, None), P()),
        out_specs=P(("ctx", "tp"), None),
        check_vma=False,
    )
```
